512 devices in a mesh: gx: 4 (over y_lo, core), gy: 4 (over x), gz: 32 (over y_hi, z).
Axes of the slice: x: 4, y: 4 (y_hi: 2, y_lo: 2; y = y_hi * 2 + y_lo), z: 16, core: 2. Of those that a mesh axis runs over, the one named last changes fastest.
Arguments:
- coarse: bfloat16 [16, 32, 8192], P('gx', 'gy', 'gz'), may hold values from -6 to 6
- skip_features: bfloat16 [32, 64, 8192], P('gx', 'gy', 'gz'), may hold values from -6 to 6
- pre_act: bfloat16 [32, 64, 8192], P('gx', 'gy', 'gz'), may hold values from -9 to 9
- cotangent: bfloat16 [3, 32, 64, 128], P(None, 'gx', 'gy', 'gz'), may hold values from -24 to 24
- weight_one: bfloat16 [27, 12288], replicated, may hold values from -0.078125 to 0.078125
- weight_out: bfloat16 [27, 3, 64], replicated, may hold values from -0.15625 to 0.15625
Outputs:
- coarse_grad: bfloat16 [16, 32, 8192], P('gx', 'gy', 'gz')
- skip_grad: bfloat16 [32, 64, 8192], P('gx', 'gy', 'gz')
- weight_one_grad: float32 [27, 12288], replicated
- weight_out_grad: float32 [27, 3, 64], replicated
The draws below stay inside these ranges and needn't reach their ends.
All inputs are finite; a program needn't handle non-finite values.
Results may differ from the reference program's by a relative error of at most 0.0049.
Values may be sent and summed in bfloat16 or wider, within the bound.
No kernel may reach another device: no remote copies, remote signals or barrier semaphores. Data moves between devices by JAX's collectives and lax.ppermute only.
A program may use at most 64 MiB of HBM per device.

```python
import math
import jax
import jax.numpy as jnp
from jax import lax

C_UP = 128
C_HID = 64
C_VEL = 3
TAPS = 27
CX = 8
C_IN = 192
NX = 32
NY = 64
NZ = 128


def block_scale(stream_key, shape, cuts, smallest, largest):
    factor_of, own = 1.0, jax.random.fold_in(stream_key, 6)
    for position, blocks in cuts:
        steps = jnp.exp(jax.random.uniform(jax.random.fold_in(own, position), (blocks,), jnp.float32, smallest / len(cuts), largest / len(cuts)))
        factor_of = factor_of * jnp.repeat(steps, shape[position] // blocks).reshape([-1 if axis == position else 1 for axis in range(len(shape))])
    return factor_of


def scatter_about(own_key, dims, spread, most, cuts=(), held_as=jnp.bfloat16):
    array = jax.random.normal(own_key, dims, jnp.float32) * spread
    if len(cuts) > 0:
        array = block_scale(own_key, dims, cuts, -0.22, 0.18) * array
    return jnp.clip(array, min=-most, max=most).astype(held_as)


def setup_inputs(seed: int = 0) -> dict:
    splits = jax.random.split(jax.random.key(seed), 7)
    return {
        "coarse": scatter_about(splits[0], (NX // 2, NY // 2, NZ // 2 * C_UP), 1.0, 6.0, ((0, 4), (1, 4), (2, 32))),
        "skip_features": scatter_about(splits[1], (NX, NY, NZ * C_HID), 1.0, 6.0, ((0, 4), (1, 4), (2, 32))),
        "pre_act": scatter_about(splits[2], (NX, NY, NZ * C_HID), 1.5, 9.0, ((0, 4), (1, 4), (2, 32))),
        "cotangent": scatter_about(splits[3], (C_VEL, NX, NY, NZ), 4.0, 24.0, ((1, 4), (2, 4), (3, 32))),
        "weight_one": scatter_about(splits[4], (TAPS, C_HID * C_IN), (TAPS * C_IN) ** -0.5, 0.078125),
        "weight_out": scatter_about(splits[5], (TAPS, C_VEL, C_HID), (TAPS * C_HID) ** -0.5, 0.15625),
    }


root_half = 0.7071067811865476
inv_root_tau = 0.3989422804014327

def gelu_value(values):
    return 0.5 * values * (1.0 + lax.erf(values * root_half))

def gelu_slope(values):
    return 0.5 * (1.0 + lax.erf(values * root_half)) + values * jnp.exp(-0.5 * values * values) * inv_root_tau

def to_channels(packed, channels):
    shaped = packed.reshape(packed.shape[0], packed.shape[1], packed.shape[2] // channels, channels)
    return jnp.transpose(shaped, (3, 0, 1, 2))

def from_channels(field):
    moved = jnp.transpose(field, (1, 2, 3, 0))
    return moved.reshape(moved.shape[0], moved.shape[1], moved.shape[2] * moved.shape[3])

def upsample(coarse):
    doubled = jnp.repeat(coarse, 2, axis=1)
    doubled = jnp.repeat(doubled, 2, axis=2)
    return jnp.repeat(doubled, 2, axis=3)

def window_at(padded, shift_x, shift_y, shift_z, grid_shape):
    size_x, size_y, size_z = grid_shape
    cut_piece = padded[:, 1 + shift_x:1 + shift_x + size_x, 1 + shift_y:1 + shift_y + size_y, 1 + shift_z:1 + shift_z + size_z]
    return cut_piece.reshape(padded.shape[0], size_x * size_y * size_z)

def stacked_taps(padded, direction, shift_x, grid_shape):
    return jnp.concatenate([window_at(padded, direction * shift_x, direction * shift_y, direction * shift_z, grid_shape) for shift_y in (-1, 0, 1) for shift_z in (-1, 0, 1)], axis=0)

def contract_rows(left_side, right_side):
    return lax.dot_general(left_side, right_side, (((0,), (0,)), ((), ())), preferred_element_type=jnp.float32)

def contract_cells(left_side, right_side):
    return lax.dot_general(left_side, right_side, (((1,), (1,)), ((), ())), preferred_element_type=jnp.float32)

def extend_x(grid_field):
    return jnp.concatenate([grid_field[:, -1:], grid_field, grid_field[:, :1]], axis=1)

def wrap_sides(block_field):
    return jnp.pad(block_field, ((0, 0), (0, 0), (1, 1), (1, 1)), mode='wrap')

def reference(coarse, skip_features, pre_act, cotangent, weight_one, weight_out):
    tap_count = weight_out.shape[0]
    hid_channels = weight_out.shape[2]
    vel_channels = cotangent.shape[0]
    up_channels = C_UP
    coarse = to_channels(coarse, up_channels)
    skip_features = to_channels(skip_features, hid_channels)
    pre_act = to_channels(pre_act, hid_channels)
    weight_one = weight_one.reshape(tap_count, hid_channels, weight_one.shape[1] // hid_channels)
    blocks = NX // CX
    grid_shape = (CX, NY, NZ)
    cell_count = CX * NY * NZ
    extended_cot = extend_x(cotangent)
    head_rows = weight_out.reshape(tap_count * vel_channels, hid_channels)

    def first_pass(running, block_index):
        block_start = block_index * CX
        rim_cot = wrap_sides(lax.dynamic_slice_in_dim(extended_cot, block_start, CX + 2, 1))
        pre_block = lax.dynamic_slice_in_dim(pre_act, block_start, CX, 1).astype(jnp.float32).reshape(hid_channels, cell_count)
        hidden = gelu_value(pre_block).astype(jnp.bfloat16)
        cot_back = jnp.concatenate([stacked_taps(rim_cot, -1, shift_x, grid_shape) for shift_x in (-1, 0, 1)], axis=0)
        d_hidden = contract_rows(head_rows, cot_back)
        d_pre = (d_hidden * gelu_slope(pre_block)).astype(jnp.bfloat16)
        running = running + contract_cells(cot_back, hidden).reshape(tap_count, vel_channels, hid_channels)
        return (running, d_pre.reshape(hid_channels, CX, NY, NZ))
    out_zero = jnp.zeros((tap_count, vel_channels, hid_channels), jnp.float32)
    head_grad, pre_blocks = lax.scan(first_pass, out_zero, jnp.arange(blocks, dtype=jnp.int32))
    d_pre_all = jnp.moveaxis(pre_blocks, 0, 1).reshape(hid_channels, NX, NY, NZ)
    inputs = jnp.concatenate([upsample(coarse), skip_features], axis=0)
    in_channels = inputs.shape[0]
    extended_pre = extend_x(d_pre_all)

    def second_pass(running, block_index):
        block_start = block_index * CX
        rim_pre = wrap_sides(lax.dynamic_slice_in_dim(extended_pre, block_start, CX + 2, 1))
        in_block = lax.dynamic_slice_in_dim(inputs, block_start, CX, 1).reshape(in_channels, cell_count)
        d_input = jnp.zeros((in_channels, cell_count), jnp.float32)
        pieces = []
        for group_index, shift_x in enumerate((-1, 0, 1)):
            pre_back = stacked_taps(rim_pre, -1, shift_x, grid_shape)
            tap_rows = weight_one[9 * group_index:9 * group_index + 9].reshape(9 * hid_channels, in_channels)
            d_input = d_input + contract_rows(tap_rows, pre_back)
            pieces.append(contract_cells(pre_back, in_block).reshape(9, hid_channels, in_channels))
        running = running + jnp.concatenate(pieces, axis=0)
        skip_block = d_input[up_channels:].reshape(in_channels - up_channels, CX, NY, NZ).astype(jnp.bfloat16)
        coarse_block = d_input[:up_channels].reshape(up_channels, CX // 2, 2, NY // 2, 2, NZ // 2, 2).sum(axis=(2, 4, 6)).astype(jnp.bfloat16)
        return (running, (coarse_block, skip_block))
    one_zero = jnp.zeros((tap_count, hid_channels, in_channels), jnp.float32)
    body_grad, outputs = lax.scan(second_pass, one_zero, jnp.arange(blocks, dtype=jnp.int32))
    coarse_blocks, skip_blocks = outputs
    coarse_grad = jnp.moveaxis(coarse_blocks, 0, 1).reshape(up_channels, NX // 2, NY // 2, NZ // 2)
    skip_grad = jnp.moveaxis(skip_blocks, 0, 1).reshape(in_channels - up_channels, NX, NY, NZ)
    norm_factor = 1.0 / math.sqrt(NX * NY * NZ)
    body_out = (body_grad * norm_factor).reshape(tap_count, hid_channels * in_channels)
    return (from_channels(coarse_grad), from_channels(skip_grad), body_out, head_grad * norm_factor)
```

```python
import math

import jax
import jax.numpy as jnp
from jax import lax
from jax.sharding import PartitionSpec as P

C_UP = 128


root_half = 0.7071067811865476
inv_root_tau = 0.3989422804014327


def extended(array, sides, width):
    for axis, dim in sides:
        peers, length = (lax.axis_size(axis), array.shape[dim])
        up = [(i, (i + 1) % peers) for i in range(peers)]
        down = [(j, i) for i, j in up]
        last = lax.slice_in_dim(array, length - width, length, axis=dim)
        first = lax.slice_in_dim(array, 0, width, axis=dim)
        before = lax.ppermute(last, axis, up)
        after = lax.ppermute(first, axis, down)
        array = jnp.concatenate([before, array, after], axis=dim)
    return array


def gelu_value(values):
    return 0.5 * values * (1.0 + lax.erf(values * root_half))


def gelu_slope(values):
    return (
        0.5 * (1.0 + lax.erf(values * root_half))
        + values * jnp.exp(-0.5 * values * values) * inv_root_tau
    )


def to_channels(packed, channels):
    shaped = packed.reshape(packed.shape[0], packed.shape[1], packed.shape[2] // channels, channels)
    return jnp.transpose(shaped, (3, 0, 1, 2))


def from_channels(field):
    moved = jnp.transpose(field, (1, 2, 3, 0))
    return moved.reshape(moved.shape[0], moved.shape[1], moved.shape[2] * moved.shape[3])


def upsample(coarse):
    doubled = jnp.repeat(coarse, 2, axis=1)
    doubled = jnp.repeat(doubled, 2, axis=2)
    return jnp.repeat(doubled, 2, axis=3)


def window_at(padded, shift_x, shift_y, shift_z, grid_shape):
    size_x, size_y, size_z = grid_shape
    cut_piece = padded[
        :,
        1 + shift_x : 1 + shift_x + size_x,
        1 + shift_y : 1 + shift_y + size_y,
        1 + shift_z : 1 + shift_z + size_z,
    ]
    return cut_piece.reshape(padded.shape[0], size_x * size_y * size_z)


def stacked_taps(padded, direction, shift_x, grid_shape):
    return jnp.concatenate(
        [
            window_at(
                padded, direction * shift_x, direction * shift_y, direction * shift_z, grid_shape
            )
            for shift_y in (-1, 0, 1)
            for shift_z in (-1, 0, 1)
        ],
        axis=0,
    )


def contract_rows(left_side, right_side):
    return lax.dot_general(
        left_side, right_side, (((0,), (0,)), ((), ())), preferred_element_type=jnp.float32
    )


def contract_cells(left_side, right_side):
    return lax.dot_general(
        left_side, right_side, (((1,), (1,)), ((), ())), preferred_element_type=jnp.float32
    )


def grad_rims(grid_field):
    return extended(grid_field, (("gx", 1), ("gy", 2), ("gz", 3)), 1)


def packed_parts(body_grad, head_grad, parts, rows):
    body = body_grad.reshape(parts, -1)
    head = head_grad.reshape(parts, -1)
    room = rows * 128 - body.shape[1] - head.shape[1]
    flat = jnp.concatenate([body, head, jnp.zeros((parts, room), jnp.float32)], axis=1)
    return flat.reshape(parts, rows, 128)


def sum_everywhere(body_grad, head_grad):
    plane = ("gx", "gy")
    parts = lax.axis_size("gx") * lax.axis_size("gy")
    deep = lax.axis_size("gz")
    per_part = (body_grad.size + head_grad.size) // parts
    rows = -(-per_part // (128 * deep)) * deep
    packed = packed_parts(body_grad, head_grad, parts, rows).astype(jnp.bfloat16)
    traded = lax.all_to_all(packed, plane, 0, 0)
    mine = jnp.sum(traded.astype(jnp.float32), axis=0)
    deep_parts = mine.reshape(deep, rows // deep, 128)
    deep_traded = lax.all_to_all(deep_parts, "gz", 0, 0)
    total = jnp.sum(deep_traded, axis=0).astype(jnp.bfloat16)
    column = lax.all_gather(total, "gz", axis=0, tiled=True)
    full = lax.all_gather(column, plane, axis=0)
    flat = full.reshape(parts, rows * 128).astype(jnp.float32)
    body_part = body_grad.size // parts
    head_part = head_grad.size // parts
    body = flat[:, :body_part].reshape(body_grad.shape)
    head = flat[:, body_part : body_part + head_part].reshape(head_grad.shape)
    return body, head


def per_device(coarse, skip_features, pre_act, cotangent, weight_one, weight_out):
    tap_count = weight_out.shape[0]
    hid_channels = weight_out.shape[2]
    vel_channels = cotangent.shape[0]
    up_channels = C_UP
    coarse = to_channels(coarse, up_channels)
    skip_features = to_channels(skip_features, hid_channels)
    pre_act = to_channels(pre_act, hid_channels)
    weight_one = weight_one.reshape(tap_count, hid_channels, weight_one.shape[1] // hid_channels)
    grid_shape = skip_features.shape[1:]
    cell_count = grid_shape[0] * grid_shape[1] * grid_shape[2]
    in_channels = up_channels + hid_channels
    pre_float = pre_act.astype(jnp.float32).reshape(hid_channels, cell_count)
    hidden = gelu_value(pre_float).astype(jnp.bfloat16)
    rim_cot = grad_rims(cotangent)
    cot_back = jnp.concatenate(
        [stacked_taps(rim_cot, -1, shift_x, grid_shape) for shift_x in (-1, 0, 1)], axis=0
    )
    d_hidden = contract_rows(weight_out.reshape(tap_count * vel_channels, hid_channels), cot_back)
    head_grad = contract_cells(cot_back, hidden).reshape(tap_count, vel_channels, hid_channels)
    d_pre = (d_hidden * gelu_slope(pre_float)).astype(jnp.bfloat16)
    rim_pre = grad_rims(d_pre.reshape(hid_channels, *grid_shape))
    d_input = jnp.zeros((in_channels, cell_count), jnp.float32)
    fine_coarse = upsample(coarse)
    inputs = jnp.concatenate([fine_coarse, skip_features], axis=0).reshape(in_channels, cell_count)
    body_parts = []
    for group_index, shift_x in enumerate((-1, 0, 1)):
        pre_back = stacked_taps(rim_pre, -1, shift_x, grid_shape)
        tap_rows = weight_one[9 * group_index : 9 * group_index + 9].reshape(
            9 * hid_channels, in_channels
        )
        d_input = d_input + contract_rows(tap_rows, pre_back)
        body_parts.append(
            contract_cells(pre_back, inputs).reshape(9, hid_channels, in_channels)
        )
    body_grad = jnp.concatenate(body_parts, axis=0)
    summed_body, summed_head = sum_everywhere(body_grad, head_grad)
    total_cells = cell_count * lax.axis_size("gx") * lax.axis_size("gy") * lax.axis_size("gz")
    norm_factor = 1.0 / math.sqrt(total_cells)
    size_x, size_y, size_z = grid_shape
    skip_grad = (
        d_input[up_channels:]
        .reshape(in_channels - up_channels, size_x, size_y, size_z)
        .astype(jnp.bfloat16)
    )
    coarse_grad = (
        d_input[:up_channels]
        .reshape(up_channels, size_x // 2, 2, size_y // 2, 2, size_z // 2, 2)
        .sum(axis=(2, 4, 6))
        .astype(jnp.bfloat16)
    )
    body_out = (summed_body * norm_factor).reshape(tap_count, hid_channels * in_channels)
    return (
        from_channels(coarse_grad),
        from_channels(skip_grad),
        body_out,
        summed_head * norm_factor,
    )


def solution(mesh):
    in_specs = (
        P("gx", "gy", "gz"),
        P("gx", "gy", "gz"),
        P("gx", "gy", "gz"),
        P(None, "gx", "gy", "gz"),
        P(),
        P(),
    )
    out_specs = (P("gx", "gy", "gz"), P("gx", "gy", "gz"), P(), P())
    return jax.shard_map(
        per_device, mesh=mesh, in_specs=in_specs, out_specs=out_specs, check_vma=False
    )
```

```python
import jax
import jax.numpy as jnp
from jax import lax
from jax.experimental import pallas as pl
from jax.experimental.pallas import tpu as pltpu
from jax.sharding import Mesh, PartitionSpec as P

C_UP = 128
C_HID = 64
C_VEL = 3
SIZE_X, SIZE_Y, SIZE_Z = 8, 16, 4
CELLS = SIZE_X * SIZE_Y * SIZE_Z
NORM = 1.0 / 512.0
F32, BF16 = jnp.float32, jnp.bfloat16

GZ = ("gzh", "gzm", "gzl")
FIRST = ("gx", "gyl")
SECOND = ("gyh", "gzl")
THIRD = ("gzh", "gzm")
PACK_ROWS = 3072
TAP_ROWS = 336

root_half = 0.7071067811865476
inv_root_tau = 0.3989422804014327


def gelu_value(values):
    return 0.5 * values * (1.0 + lax.erf(values * root_half))


def gelu_slope(values):
    return (
        0.5 * (1.0 + lax.erf(values * root_half))
        + values * jnp.exp(-0.5 * values * values) * inv_root_tau
    )


def from_both(to_next, to_previous, axis):
    peers = lax.axis_size(axis)
    up = [(i, (i + 1) % peers) for i in range(peers)]
    down = [(j, i) for i, j in up]
    return lax.ppermute(to_next, axis, up), lax.ppermute(to_previous, axis, down)


def extended_fields(pre_act, cotangent):
    cot = jnp.transpose(cotangent, (1, 2, 3, 0)).reshape(SIZE_X, SIZE_Y, SIZE_Z * C_VEL)
    fill = jnp.zeros((SIZE_X, SIZE_Y, 58), BF16)
    high = jnp.concatenate([pre_act[..., 192:], cot[..., 6:], fill], axis=-1)
    low = jnp.concatenate([pre_act[..., :64], cot[..., :6], fill], axis=-1)
    before, after = from_both(high, low, GZ)
    fill = jnp.zeros((SIZE_X, SIZE_Y, 104), BF16)
    field = jnp.concatenate(
        [before[..., :64], pre_act, after[..., :64], before[..., 64:70], cot, after[..., 64:70], fill],
        axis=-1,
    )
    before, after = from_both(field[6:], field[:2], "gx")
    field = jnp.concatenate([before, field, after], axis=0)
    before, after = from_both(field[:, 14:], field[:, :2], ("gyh", "gyl"))
    fill = jnp.zeros((SIZE_X + 4, 12, 512), BF16)
    return jnp.concatenate([before, field, after, fill], axis=1)


def head_matrix(weight_out):
    taps = weight_out.reshape(9, 3, C_VEL, C_HID)[:, ::-1].reshape(9, 9, C_HID)
    columns = [jnp.pad(taps, ((0, 0), (3 * z, 23 - 3 * z), (0, 0))) for z in range(6)]
    return jnp.concatenate(columns, axis=2)


def input_matrix(weight_one):
    taps = weight_one.reshape(9, 3, C_HID, 192)[:, ::-1].reshape(9, 192, 192)
    wide = jnp.concatenate([taps, taps[..., C_UP:]], axis=2)
    return jnp.pad(wide, ((0, 0), (0, 64), (0, 0)))


def low_half(shape):
    return lax.broadcasted_iota(jnp.int32, shape, len(shape) - 1) < 64


def rolled(values, shift):
    flat = values.reshape(-1, values.shape[-1])
    return pltpu.roll(flat, shift, 1).reshape(values.shape)


def gradient_kernel(
    field_ref, pre_ref, skip_ref, coarse_ref, head_ref, pack_ref, window_ref, cot_s, pre_s, in_s
):
    cot_s[:, 0:8, :] = jnp.zeros((12, 8, 128), F32)
    cot_s[:, 8:40, :] = field_ref[:, :, 384:512].astype(F32)
    total = jnp.zeros((240, 384), F32)
    for a in (-1, 0, 1):
        for b in (-1, 0, 1):
            moved = cot_s[1 - a : 11 - a, 8 - b : 32 - b, :].reshape(240, 128).astype(BF16)
            total = total + jnp.dot(
                moved[:, :32], head_ref[3 * (a + 1) + b + 1], preferred_element_type=F32
            )
    pre_wide = field_ref[1:11, :, 0:384].astype(F32)[:, :24].reshape(240, 384)
    d_pre = (total * gelu_slope(pre_wide)).astype(BF16).astype(F32)
    pre_s[:, :, 0:384] = d_pre.reshape(10, 24, 384)
    pre_s[:, :, 384:512] = cot_s[1:11, 8:32, :]

    half = low_half((10, 16, 128))
    for b in (-1, 0, 1):
        moved = pre_s[:, 2 - b : 18 - b, :]
        shifted = rolled(moved[:, :, :384], 320)
        for z in range(SIZE_Z):
            source, start = (moved, 64 * z) if z % 2 == 0 else (shifted, 64 * z - 64)
            low = source[:, :, start : start + 128]
            high = source[:, :, start + 128 : start + 256]
            cot = rolled(moved[:, :, 384:512], 61 - 3 * z)
            window_ref[b + 1, z, :, :, 0:128] = low.astype(BF16)
            window_ref[b + 1, z, :, :, 128:256] = jnp.where(half, high, cot).astype(BF16)

    hidden = gelu_value(pre_ref[...].astype(F32))
    skip = skip_ref[...].astype(F32)
    half = low_half((8, 16, 128))
    for z in range(SIZE_Z):
        pair = slice(128 * (z // 2), 128 * (z // 2) + 128)
        if z % 2 == 0:
            second = jnp.where(half, skip[:, :, pair], rolled(hidden[:, :, pair], 64))
        else:
            second = jnp.where(half, rolled(skip[:, :, pair], 64), hidden[:, :, pair])
        in_s[z, :, :, 128:256] = second.astype(BF16)
        for x in range(SIZE_X):
            in_s[z, x, :, 0:128] = coarse_ref[x // 2, :, pair]

    inputs = in_s[...].reshape(CELLS, 256)
    half = low_half((64, 128))
    for a in (-1, 0, 1):
        for b in (-1, 0, 1):
            window = window_ref[b + 1, :, 1 - a : 9 - a].reshape(CELLS, 256)
            result = lax.dot_general(
                window, inputs, (((0,), (0,)), ((), ())), preferred_element_type=F32
            )
            start = TAP_ROWS * (3 * (a + 1) + b + 1)
            pair = jnp.where(half, result[0:64, 128:256], rolled(result[64:128, 128:256], 64))
            pack_ref[start : start + 192, :] = result[0:192, 0:128].astype(BF16)
            pack_ref[start + 192 : start + 256, :] = pair.astype(BF16)
            pack_ref[start + 256 : start + 336, :] = result[128:208, 128:256].astype(BF16)
    pack_ref[9 * TAP_ROWS : PACK_ROWS, :] = jnp.zeros((PACK_ROWS - 9 * TAP_ROWS, 128), BF16)


def input_kernel(window_ref, weight_ref, skip_ref, coarse_ref, sum_s):
    windows = [
        window_ref[b + 1, :, 1 - a : 9 - a].reshape(CELLS, 256)
        for a in (-1, 0, 1)
        for b in (-1, 0, 1)
    ]
    total = jnp.dot(
        jnp.concatenate(windows, axis=1),
        weight_ref[...].reshape(9 * 256, 256),
        preferred_element_type=F32,
    ).reshape(SIZE_Z, SIZE_X, SIZE_Y, 256)
    half = low_half((8, 16, 128))
    for pair in range(2):
        even, odd = total[2 * pair], total[2 * pair + 1]
        lanes = slice(128 * pair, 128 * pair + 128)
        skip_ref[:, :, lanes] = jnp.where(half, even[..., 128:], odd[..., 128:]).astype(BF16)
        both = (even[..., :128] + odd[..., :128]).reshape(4, 2, 16, 128)
        sum_s[...] = (both[:, 0] + both[:, 1]).reshape(64, 128)
        summed = sum_s[pl.ds(0, 32, stride=2), :] + sum_s[pl.ds(1, 32, stride=2), :]
        coarse_ref[:, lanes] = summed.astype(BF16)


def traded(parts, axes):
    return lax.all_to_all(parts, axes, 0, 0)


def spread(part, axes):
    peers = lax.axis_size(axes)
    return traded(jnp.broadcast_to(part[None], (peers, *part.shape)), axes)


def sum_everywhere(packed):
    first = traded(packed.reshape(8, 384, 128), FIRST)
    first = jnp.sum(first.astype(F32), axis=0)
    second = jnp.sum(traded(first.reshape(8, 48, 128), SECOND), axis=0)
    third = jnp.sum(spread(second, THIRD), axis=0)
    fourth = spread(third.astype(BF16), SECOND).reshape(384, 128)
    return spread(fourth, FIRST).reshape(PACK_ROWS, 128)


def unpacked(packed):
    taps = packed[: 9 * TAP_ROWS].reshape(9, TAP_ROWS, 128).astype(F32) * NORM
    up = taps[:, :192].reshape(9, 3, C_HID, C_UP)
    pair = taps[:, 192:256]
    third = taps[:, 256:320, :64]
    skip = jnp.stack([pair[..., :64], pair[..., 64:], third], axis=1)
    body = jnp.concatenate([up, skip], axis=-1)[:, ::-1].reshape(27, C_HID * 192)
    head = taps[:, 320:329, 64:].reshape(9, 3, C_VEL, C_HID)[:, ::-1].reshape(27, C_VEL, C_HID)
    return body, head


def per_device(coarse, skip_features, pre_act, cotangent, weight_one, weight_out):
    field = extended_fields(pre_act, cotangent)
    packed, window = pl.pallas_call(
        gradient_kernel,
        out_shape=(
            jax.ShapeDtypeStruct((PACK_ROWS, 128), BF16),
            jax.ShapeDtypeStruct((3, SIZE_Z, 10, 16, 256), BF16),
        ),
        scratch_shapes=[
            pltpu.VMEM((12, 40, 128), F32),
            pltpu.VMEM((10, 24, 512), F32),
            pltpu.VMEM((SIZE_Z, SIZE_X, SIZE_Y, 256), BF16),
        ],
        compiler_params=pltpu.CompilerParams(vmem_limit_bytes=32 * 2**20),
        cost_estimate=pl.CostEstimate(
            flops=700_000_000, bytes_accessed=3_000_000, transcendentals=200_000
        ),
    )(field, pre_act, skip_features, jnp.repeat(coarse, 2, axis=1), head_matrix(weight_out))
    skip_grad, coarse_grad = pl.pallas_call(
        input_kernel,
        out_shape=(
            jax.ShapeDtypeStruct((SIZE_X, SIZE_Y, 256), BF16),
            jax.ShapeDtypeStruct((32, 256), BF16),
        ),
        scratch_shapes=[pltpu.VMEM((64, 128), F32)],
        compiler_params=pltpu.CompilerParams(vmem_limit_bytes=32 * 2**20),
        cost_estimate=pl.CostEstimate(
            flops=700_000_000, bytes_accessed=3_000_000, transcendentals=0
        ),
    )(window, input_matrix(weight_one))
    body, head = unpacked(sum_everywhere(packed))
    return coarse_grad.reshape(4, 8, 256), skip_grad, body, head


def solution(mesh):
    names = ("gx", "gyh", "gyl", "gzh", "gzm", "gzl")
    split = Mesh(mesh.devices.reshape(4, 2, 2, 2, 4, 4), names)
    field = P("gx", ("gyh", "gyl"), GZ)
    return jax.shard_map(
        per_device,
        mesh=split,
        in_specs=(field, field, field, P(None, "gx", ("gyh", "gyl"), GZ), P(), P()),
        out_specs=(field, field, P(), P()),
        check_vma=False,
    )
```

```python
import jax
import jax.numpy as jnp
import numpy as np
from jax import lax
from jax.experimental import pallas as pl
from jax.experimental.pallas import tpu as pltpu
from jax.sharding import Mesh, PartitionSpec as P

C_UP = 128
C_HID = 64
C_VEL = 3
SIZE_X, SIZE_Y, SIZE_Z = 8, 16, 4
CELLS = SIZE_X * SIZE_Y * SIZE_Z
NORM = 1.0 / 512.0
F32, BF16 = jnp.float32, jnp.bfloat16

GX, GY, GZ = "gx", "gy", ("gzh", "gzm", "gzl")
PLANE = ("gx", "gy")
NEAR = ("gzh", "gzl")
FAR = "gzm"
BLOCKS = 16
OWN = C_HID // BLOCKS
ROWS = 6 * OWN
SHARE = (32, OWN * 192)
HIGHEST = lax.Precision.HIGHEST


root_half = 0.7071067811865476
inv_root_tau = 0.3989422804014327


def gelu_value(values):
    return 0.5 * values * (1.0 + lax.erf(values * root_half))


def gelu_slope(values):
    return (
        0.5 * (1.0 + lax.erf(values * root_half))
        + values * jnp.exp(-0.5 * values * values) * inv_root_tau
    )


def from_both(to_next, to_previous, axis):
    peers = lax.axis_size(axis)
    up = [(i, (i + 1) % peers) for i in range(peers)]
    down = [(j, i) for i, j in up]
    return lax.ppermute(to_next, axis, up), lax.ppermute(to_previous, axis, down)


def depth_rims(pre_act, cotangent):
    pre = pre_act.reshape(128, SIZE_Z * C_HID).T
    cot = jnp.transpose(cotangent, (3, 0, 1, 2)).reshape(SIZE_Z * C_VEL, 128)
    fill = jnp.zeros((10, 128), BF16)
    high = jnp.concatenate([pre[192:], cot[6:], fill], axis=0)
    low = jnp.concatenate([pre[:64], cot[:6], fill], axis=0)
    before, after = from_both(high, low, GZ)
    pre = jnp.concatenate([before[:64], pre, after[:64]], axis=0)
    cot = jnp.concatenate([before[64:70], cot, after[64:70]], axis=0)
    return pre, cot


def plane_shares(pre, cot):
    own = jnp.transpose(pre.reshape(6, BLOCKS, OWN, 128), (1, 0, 2, 3)).reshape(BLOCKS, ROWS, 128)
    parts = jnp.concatenate([own, jnp.broadcast_to(cot[None], (BLOCKS, 24, 128))], axis=1)
    return traded(parts, PLANE)


def plane_inputs(coarse, skip_features):
    part = jnp.concatenate([coarse.reshape(32, 256), skip_features.reshape(128, 256)], axis=0)
    return spread(part, PLANE)


def side_field(pre, cot):
    fill = jnp.zeros((104, 128), BF16)
    return jnp.concatenate([pre, cot, fill], axis=0).T.reshape(SIZE_X, SIZE_Y, 512)


def with_x_rims(field):
    before, after = from_both(field[6:], field[:2], GX)
    return jnp.concatenate([before, field, after], axis=0)


def with_y_rims(field):
    before, after = from_both(field[:, 14:], field[:, :2], GY)
    fill = jnp.zeros((SIZE_X + 4, 12, 512), BF16)
    return jnp.concatenate([before, field, after, fill], axis=1)


def head_matrix(weight_out):
    taps = weight_out.reshape(9, 3, C_VEL, C_HID)[:, ::-1].reshape(9, 9, C_HID)
    columns = [jnp.pad(taps, ((0, 0), (3 * z, 23 - 3 * z), (0, 0))) for z in range(6)]
    return jnp.concatenate(columns, axis=2)


def own_head_matrix(head):
    place = lax.axis_index(GX) * lax.axis_size(GY) + lax.axis_index(GY)
    split = head[:, :24].reshape(9, 24, 6, BLOCKS, OWN)
    own = lax.dynamic_index_in_dim(split, place, 3, keepdims=False)
    return jnp.transpose(own, (2, 3, 0, 1)).reshape(ROWS, 216)


def choices():
    tap_rows = np.zeros((2, 2, OWN, 32, 216), np.float32)
    head_columns = np.zeros((9, 8, C_VEL, SIZE_Z, 128), np.float32)
    for tap in range(27):
        pair, c = tap // 3, tap % 3 - 1
        for z in range(SIZE_Z):
            for own in range(OWN):
                row = ROWS * pair + OWN * (z + 1 - c) + own
                tap_rows[z // 2, z % 2, own, tap, row] = 1.0
            for o in range(C_VEL):
                head_columns[pair, z + 2 - c, o, z, C_VEL * tap + o] = 1.0
    head_rows = np.zeros((32, 6, OWN), np.float32)
    for own in range(OWN):
        head_rows[27 + own, 1:5, own] = 1.0
    double = np.zeros((SIZE_X, SIZE_Y, SIZE_X // 2, SIZE_Y // 2), np.float32)
    for x in range(SIZE_X):
        for y in range(SIZE_Y):
            double[x, y, x // 2, y // 2] = 1.0
    return (
        jnp.asarray(tap_rows.reshape(2, 256, 216), BF16),
        jnp.asarray(head_columns.reshape(216, 512)),
        jnp.asarray(head_rows.reshape(32, ROWS)),
        jnp.asarray(double.reshape(128, 32), BF16),
    )


def input_matrix(weight_one):
    taps = weight_one.reshape(9, 3, C_HID, 192)[:, ::-1].reshape(9, 192, 192)
    wide = jnp.concatenate([taps, taps[..., C_UP:]], axis=2)
    return jnp.pad(wide, ((0, 0), (0, 64), (0, 0)))


def low_half(shape):
    return lax.broadcasted_iota(jnp.int32, shape, len(shape) - 1) < 64


def rolled(values, shift):
    flat = values.reshape(-1, values.shape[-1])
    return pltpu.roll(flat, shift, 1).reshape(values.shape)


def moved_y(blocks, b, lane):
    if b == 0:
        return blocks
    out = []
    for at in range(BLOCKS):
        gx, gy = at // 4, at % 4
        there = blocks[4 * gx + (gy - b) % 4]
        edge = lane % 16 == (0 if b == 1 else 15)
        out.append(
            jnp.where(edge, pltpu.roll(there, -15 * b % 128, 1), pltpu.roll(blocks[at], b % 128, 1))
        )
    return out


def moved_x(blocks, a, lane):
    if a == 0:
        return blocks
    turned = [pltpu.roll(block, 16 * a % 128, 1) for block in blocks]
    edge = lane // 16 == (0 if a == 1 else 7)
    return [
        jnp.where(edge, turned[4 * ((at // 4 - a) % 4) + at % 4], turned[at])
        for at in range(BLOCKS)
    ]


def stack_moved(blocks, stack_ref):
    lane = lax.broadcasted_iota(jnp.int32, (ROWS, 128), 1)
    for b in (-1, 0, 1):
        rows = moved_y(blocks, b, lane)
        for a in (-1, 0, 1):
            start = ROWS * (3 * (a + 1) + b + 1)
            for at, block in enumerate(moved_x(rows, a, lane)):
                stack_ref[start : start + ROWS, 128 * at : 128 * at + 128] = block


def share_kernel(
    data_ref, input_ref, head_ref, tap_ref, column_ref, row_ref, double_ref, share_ref, stack_s, in_s
):
    for at in range(BLOCKS):
        rows = slice(128 * at, 128 * at + 128)
        fine = jnp.dot(double_ref[...], input_ref[at, 0:32, :], preferred_element_type=F32)
        for pair in range(2):
            lanes = slice(128 * pair, 128 * pair + 128)
            in_s[pair, rows, 0:128] = fine[:, lanes].astype(BF16)
            in_s[pair, rows, 128:256] = input_ref[at, 32:160, lanes]

    blocks = [data_ref[at].astype(F32) for at in range(BLOCKS)]
    stack_moved([block[ROWS:48] for block in blocks], stack_s)
    cot = stack_s[...].astype(BF16)
    pre = jnp.concatenate([block[0:ROWS] for block in blocks], axis=1)
    d_hidden = jnp.dot(head_ref[...], cot, preferred_element_type=F32)
    d_pre = (d_hidden * gelu_slope(pre)).astype(BF16).astype(F32)
    hidden = gelu_value(pre).astype(BF16)
    pairs = lax.dot_general(hidden, cot, (((1,), (1,)), ((), ())), preferred_element_type=F32)
    spans = jnp.dot(pairs, column_ref[...], precision=HIGHEST, preferred_element_type=F32)
    depth = lax.broadcasted_iota(jnp.int32, (ROWS, 128), 0) // OWN
    kept = jnp.zeros((ROWS, 128), F32)
    for z in range(SIZE_Z):
        kept = jnp.where(depth == z + 1, spans[:, 128 * z : 128 * z + 128], kept)
    head = jnp.dot(row_ref[...], kept, precision=HIGHEST, preferred_element_type=F32)

    stack_moved([d_pre[:, 128 * at : 128 * at + 128] for at in range(BLOCKS)], stack_s)
    back = stack_s[...].astype(BF16)
    total = jnp.zeros((256, 256), F32)
    for pair in range(2):
        taps = jnp.dot(tap_ref[pair], back, preferred_element_type=F32).astype(BF16)
        total = total + jnp.dot(taps, in_s[pair], preferred_element_type=F32)
    up = total[0:128, 0:128] + total[128:256, 0:128]
    skip = total[0:128, 128:256] + rolled(total[128:256, 128:256], 64)
    half = low_half((32, 128))
    for even in range(0, OWN, 2):
        first, second = slice(32 * even, 32 * even + 32), slice(32 * even + 32, 32 * even + 64)
        turned = rolled(up[second], 64)
        start = 192 * even
        share_ref[:, start : start + 128] = up[first] + head if even == 0 else up[first]
        share_ref[:, start + 128 : start + 256] = jnp.where(half, skip[first], turned)
        share_ref[:, start + 256 : start + 384] = jnp.where(half, turned, rolled(skip[second], 64))


def input_kernel(field_ref, head_ref, weight_ref, skip_ref, coarse_ref, cot_s, pre_s, window_s, sum_s):
    cot_s[:, 0:8, :] = jnp.zeros((12, 8, 128), F32)
    cot_s[:, 8:40, :] = field_ref[:, :, 384:512].astype(F32)
    total = jnp.zeros((240, 384), F32)
    for a in (-1, 0, 1):
        for b in (-1, 0, 1):
            moved = cot_s[1 - a : 11 - a, 8 - b : 32 - b, :].reshape(240, 128).astype(BF16)
            total = total + jnp.dot(
                moved[:, :32], head_ref[3 * (a + 1) + b + 1], preferred_element_type=F32
            )
    pre_wide = field_ref[1:11, :, 0:384].astype(F32)[:, :24].reshape(240, 384)
    d_pre = (total * gelu_slope(pre_wide)).astype(BF16).astype(F32)
    pre_s[...] = d_pre.reshape(10, 24, 384)

    half = low_half((10, 16, 128))
    for b in (-1, 0, 1):
        moved = pre_s[:, 2 - b : 18 - b, :]
        shifted = rolled(moved, 320)
        for z in range(SIZE_Z):
            source, start = (moved, 64 * z) if z % 2 == 0 else (shifted, 64 * z - 64)
            low = source[:, :, start : start + 128]
            high = jnp.where(half, source[:, :, start + 128 : start + 256], 0.0)
            window_s[b + 1, z, :, :, 0:128] = low.astype(BF16)
            window_s[b + 1, z, :, :, 128:256] = high.astype(BF16)

    windows = [
        window_s[b + 1, :, 1 - a : 9 - a].reshape(CELLS, 256)
        for a in (-1, 0, 1)
        for b in (-1, 0, 1)
    ]
    total = jnp.dot(
        jnp.concatenate(windows, axis=1),
        weight_ref[...].reshape(9 * 256, 256),
        preferred_element_type=F32,
    ).reshape(SIZE_Z, SIZE_X, SIZE_Y, 256)
    half = low_half((8, 16, 128))
    for pair in range(2):
        even, odd = total[2 * pair], total[2 * pair + 1]
        lanes = slice(128 * pair, 128 * pair + 128)
        skip_ref[:, :, lanes] = jnp.where(half, even[..., 128:], odd[..., 128:]).astype(BF16)
        both = (even[..., :128] + odd[..., :128]).reshape(4, 2, 16, 128)
        sum_s[...] = (both[:, 0] + both[:, 1]).reshape(64, 128)
        summed = sum_s[pl.ds(0, 32, stride=2), :] + sum_s[pl.ds(1, 32, stride=2), :]
        coarse_ref[:, lanes] = summed.astype(BF16)


def traded(parts, axes):
    return lax.all_to_all(parts, axes, 0, 0)


def spread(part, axes):
    peers = lax.axis_size(axes)
    return traded(jnp.broadcast_to(part[None], (peers, *part.shape)), axes)


def unpacked(shares):
    wide = shares.astype(F32) * NORM
    body = jnp.transpose(wide[:, :27], (1, 0, 2)).reshape(27, C_HID * 192)
    head = wide[:, 27:31, :81].reshape(C_HID, 27, C_VEL)
    return body, jnp.transpose(head, (1, 2, 0))


def per_device(coarse, skip_features, pre_act, cotangent, weight_one, weight_out):
    inputs = plane_inputs(coarse, skip_features)
    head = head_matrix(weight_out)
    pre, cot = depth_rims(pre_act, cotangent)
    data = plane_shares(pre, cot)
    share = pl.pallas_call(
        share_kernel,
        out_shape=jax.ShapeDtypeStruct(SHARE, F32),
        scratch_shapes=[
            pltpu.VMEM((216, 2048), F32),
            pltpu.VMEM((2, 2048, 256), BF16),
        ],
        compiler_params=pltpu.CompilerParams(vmem_limit_bytes=40 * 2**20),
        cost_estimate=pl.CostEstimate(
            flops=1_500_000_000, bytes_accessed=2_000_000, transcendentals=200_000
        ),
    )(data, inputs, own_head_matrix(head), *choices())
    field = side_field(pre, cot)
    near = jnp.sum(traded(share.reshape(4, 8, SHARE[1]), NEAR), axis=0)
    field, near = lax.optimization_barrier((field, near))
    field = with_x_rims(field)
    far = jnp.sum(spread(near.astype(BF16), FAR).astype(F32), axis=0)
    column = spread(far.astype(BF16), NEAR).reshape(SHARE)
    field, column = lax.optimization_barrier((field, column))
    body, head_grad = unpacked(spread(column, PLANE))
    skip_grad, coarse_grad = pl.pallas_call(
        input_kernel,
        out_shape=(
            jax.ShapeDtypeStruct((SIZE_X, SIZE_Y, 256), BF16),
            jax.ShapeDtypeStruct((32, 256), BF16),
        ),
        scratch_shapes=[
            pltpu.VMEM((12, 40, 128), F32),
            pltpu.VMEM((10, 24, 384), F32),
            pltpu.VMEM((3, SIZE_Z, 10, 16, 256), BF16),
            pltpu.VMEM((64, 128), F32),
        ],
        compiler_params=pltpu.CompilerParams(vmem_limit_bytes=32 * 2**20),
        cost_estimate=pl.CostEstimate(
            flops=700_000_000, bytes_accessed=3_000_000, transcendentals=100_000
        ),
    )(with_y_rims(field), head, input_matrix(weight_one))
    return coarse_grad.reshape(4, 8, 256), skip_grad, body, head_grad


def solution(mesh):
    names = ("gx", "gy", "gzh", "gzm", "gzl")
    split = Mesh(mesh.devices.reshape(4, 4, 2, 8, 2), names)
    field = P("gx", "gy", GZ)
    return jax.shard_map(
        per_device,
        mesh=split,
        in_specs=(field, field, field, P(None, "gx", "gy", GZ), P(), P()),
        out_specs=(field, field, P(), P()),
        check_vma=False,
    )
```

```python
import jax
import jax.numpy as jnp
import numpy as np
from jax import lax
from jax.experimental import pallas as pl
from jax.experimental.pallas import tpu as pltpu
from jax.sharding import Mesh, PartitionSpec as P

C_UP = 128
C_HID = 64
C_VEL = 3
SIZE_X, SIZE_Y, SIZE_Z = 8, 16, 4
CELLS = SIZE_X * SIZE_Y * SIZE_Z
NORM = 1.0 / 512.0
F32, BF16 = jnp.float32, jnp.bfloat16

GX, GY, GZ = "gx", "gy", ("gzh", "gzm", "gzl")
PLANE = ("gx", "gy")
NEAR = ("gzh", "gzl")
FAR = "gzm"
BLOCKS = 16
OWN = C_HID // BLOCKS
ROWS = 6 * OWN
SHARE = (32, OWN * 192)
HIGHEST = lax.Precision.HIGHEST


root_half = 0.7071067811865476
inv_root_tau = 0.3989422804014327


def gelu_value(values):
    return 0.5 * values * (1.0 + lax.erf(values * root_half))


def gelu_slope(values):
    return (
        0.5 * (1.0 + lax.erf(values * root_half))
        + values * jnp.exp(-0.5 * values * values) * inv_root_tau
    )


def from_both(to_next, to_previous, axis):
    peers = lax.axis_size(axis)
    up = [(i, (i + 1) % peers) for i in range(peers)]
    down = [(j, i) for i, j in up]
    return lax.ppermute(to_next, axis, up), lax.ppermute(to_previous, axis, down)


def depth_rims(pre_act, cotangent):
    cot = jnp.transpose(cotangent, (3, 0, 1, 2)).reshape(SIZE_Z * C_VEL, 128)
    cot = jnp.pad(cot, ((0, 4), (0, 0)))
    rows, high, low = pl.pallas_call(
        turn_kernel,
        out_shape=(
            jax.ShapeDtypeStruct((272, 128), BF16),
            jax.ShapeDtypeStruct((80, 128), BF16),
            jax.ShapeDtypeStruct((80, 128), BF16),
        ),
    )(pre_act.reshape(128, SIZE_Z * C_HID), cot)
    before, after = from_both(high, low, GZ)
    return before, rows, after


def plane_inputs(coarse, skip_features):
    part = jnp.concatenate([coarse.reshape(32, 256), skip_features.reshape(128, 256)], axis=0)
    return spread(part, PLANE)


def with_x_rims(field):
    before, after = from_both(field[6:], field[:2], GX)
    return jnp.concatenate([before, field, after], axis=0)


def with_y_rims(field):
    before, after = from_both(field[:, 14:], field[:, :2], GY)
    fill = jnp.zeros((SIZE_X + 4, 12, 512), BF16)
    return jnp.concatenate([before, field, after, fill], axis=1)


def head_matrix(weight_out):
    taps = weight_out.reshape(9, 3, C_VEL, C_HID)[:, ::-1].reshape(9, 9, C_HID)
    columns = [jnp.pad(taps, ((0, 0), (3 * z, 23 - 3 * z), (0, 0))) for z in range(6)]
    return jnp.concatenate(columns, axis=2)


def own_head_matrix(head):
    place = lax.axis_index(GX) * lax.axis_size(GY) + lax.axis_index(GY)
    split = head[:, :24].reshape(9, 24, 6, BLOCKS, OWN)
    own = lax.dynamic_index_in_dim(split, place, 3, keepdims=False)
    return jnp.transpose(own, (2, 3, 0, 1)).reshape(ROWS, 216)


def row_choices():
    pre_at = lambda z, c: c if z < 0 else 352 + c if z > 3 else 80 + 64 * z + c
    cot_at = lambda z, o: 76 + 3 * z + o if z < 0 else 404 + 3 * z + o if z > 3 else 336 + 3 * z + o
    shares = np.zeros((BLOCKS, 48, 432), np.float32)
    lanes = np.zeros((432, 512), np.float32)
    for z in range(-1, 5):
        for c in range(C_HID):
            shares[c // OWN, OWN * (z + 1) + c % OWN, pre_at(z, c)] = 1.0
            lanes[pre_at(z, c), C_HID * (z + 1) + c] = 1.0
    for z in range(-2, 6):
        for o in range(C_VEL):
            shares[:, ROWS + C_VEL * (z + 2) + o, cot_at(z, o)] = 1.0
            lanes[cot_at(z, o), 384 + C_VEL * (z + 2) + o] = 1.0
    return jnp.asarray(shares.reshape(768, 432), BF16), jnp.asarray(lanes, BF16)


def choices():
    tap_rows = np.zeros((2, 2, OWN, 32, 216), np.float32)
    head_columns = np.zeros((9, 8, C_VEL, SIZE_Z, 128), np.float32)
    for tap in range(27):
        pair, c = tap // 3, tap % 3 - 1
        for z in range(SIZE_Z):
            for own in range(OWN):
                row = ROWS * pair + OWN * (z + 1 - c) + own
                tap_rows[z // 2, z % 2, own, tap, row] = 1.0
            for o in range(C_VEL):
                head_columns[pair, z + 2 - c, o, z, 32 * o + tap] = 1.0
    head_rows = np.zeros((32, 6, OWN), np.float32)
    for own in range(OWN):
        head_rows[27 + own, 1:5, own] = 1.0
    double = np.zeros((SIZE_X, SIZE_Y, SIZE_X // 2, SIZE_Y // 2), np.float32)
    for x in range(SIZE_X):
        for y in range(SIZE_Y):
            double[x, y, x // 2, y // 2] = 1.0
    return (
        jnp.asarray(tap_rows.reshape(2, 256, 216), BF16),
        jnp.asarray(head_columns.reshape(216, 512)),
        jnp.asarray(head_rows.reshape(32, ROWS)),
        jnp.asarray(double.reshape(128, 32), BF16),
    )


def head_channels():
    rows = np.zeros((BLOCKS, 32, C_HID), np.float32)
    for at in range(BLOCKS):
        for own in range(OWN):
            rows[at, 27 + own, OWN * at + own] = 1.0
    return jnp.asarray(rows.reshape(512, C_HID), BF16)


def turn_kernel(pre_ref, cot_ref, rows_ref, high_ref, low_ref):
    turned = pre_ref[...].astype(F32).T.astype(BF16)
    rows_ref[0:256, :] = turned
    rows_ref[256:272, :] = cot_ref[...]
    high_ref[0:64, :] = turned[192:256]
    high_ref[64:80, :] = cot_ref[...]
    low_ref[0:64, :] = turned[0:64]
    low_ref[64:80, :] = cot_ref[...]


def joined(before_ref, rows_ref, after_ref):
    return jnp.concatenate([before_ref[...], rows_ref[...], after_ref[...]], axis=0)


def parts_kernel(before_ref, rows_ref, after_ref, choice_ref, parts_ref):
    rows = joined(before_ref, rows_ref, after_ref)
    parts = jnp.dot(choice_ref[...], rows, preferred_element_type=F32)
    parts_ref[...] = parts.astype(BF16).reshape(BLOCKS, 48, 128)


def field_kernel(before_ref, rows_ref, after_ref, choice_ref, field_ref):
    turned = joined(before_ref, rows_ref, after_ref).astype(F32).T.astype(BF16)
    field = jnp.dot(turned, choice_ref[...], preferred_element_type=F32)
    field_ref[...] = field.astype(BF16).reshape(SIZE_X, SIZE_Y, 512)


def unpack_kernel(share_ref, choice_ref, body_ref, head_ref):
    for at in range(BLOCKS):
        wide = share_ref[at].astype(F32) * NORM
        body_ref[:, 768 * at : 768 * at + 768] = wide[0:27]
    rows = share_ref[:, :, 0:128].reshape(512, 128)
    head = lax.dot_general(
        rows, choice_ref[...], (((0,), (0,)), ((), ())), preferred_element_type=F32
    )
    for o in range(C_VEL):
        head_ref[:, o, :] = head[32 * o : 32 * o + 27] * NORM


def input_matrix(weight_one):
    taps = weight_one.reshape(9, 3, C_HID, 192)[:, ::-1].reshape(9, 192, 192)
    wide = jnp.concatenate([taps, taps[..., C_UP:]], axis=2)
    return jnp.pad(wide, ((0, 0), (0, 64), (0, 0)))


def low_half(shape):
    return lax.broadcasted_iota(jnp.int32, shape, len(shape) - 1) < 64


def rolled(values, shift):
    flat = values.reshape(-1, values.shape[-1])
    return pltpu.roll(flat, shift, 1).reshape(values.shape)


def moved_y(blocks, b, lane):
    if b == 0:
        return blocks
    out = []
    for at in range(BLOCKS):
        gx, gy = at // 4, at % 4
        there = blocks[4 * gx + (gy - b) % 4]
        edge = lane % 16 == (0 if b == 1 else 15)
        out.append(
            jnp.where(edge, pltpu.roll(there, -15 * b % 128, 1), pltpu.roll(blocks[at], b % 128, 1))
        )
    return out


def moved_x(blocks, a, lane):
    if a == 0:
        return blocks
    turned = [pltpu.roll(block, 16 * a % 128, 1) for block in blocks]
    edge = lane // 16 == (0 if a == 1 else 7)
    return [
        jnp.where(edge, turned[4 * ((at // 4 - a) % 4) + at % 4], turned[at])
        for at in range(BLOCKS)
    ]


def stack_moved(blocks, stack_ref):
    lane = lax.broadcasted_iota(jnp.int32, (ROWS, 128), 1)
    for b in (-1, 0, 1):
        rows = moved_y(blocks, b, lane)
        for a in (-1, 0, 1):
            start = ROWS * (3 * (a + 1) + b + 1)
            for at, block in enumerate(moved_x(rows, a, lane)):
                stack_ref[start : start + ROWS, 128 * at : 128 * at + 128] = block


def share_kernel(
    data_ref, input_ref, head_ref, tap_ref, column_ref, row_ref, double_ref, share_ref, stack_s, in_s
):
    for at in range(BLOCKS):
        rows = slice(128 * at, 128 * at + 128)
        fine = jnp.dot(double_ref[...], input_ref[at, 0:32, :], preferred_element_type=F32)
        for pair in range(2):
            lanes = slice(128 * pair, 128 * pair + 128)
            in_s[pair, rows, 0:128] = fine[:, lanes].astype(BF16)
            in_s[pair, rows, 128:256] = input_ref[at, 32:160, lanes]

    blocks = [data_ref[at].astype(F32) for at in range(BLOCKS)]
    stack_moved([block[ROWS:48] for block in blocks], stack_s)
    cot = stack_s[...].astype(BF16)
    pre = jnp.concatenate([block[0:ROWS] for block in blocks], axis=1)
    d_hidden = jnp.dot(head_ref[...], cot, preferred_element_type=F32)
    d_pre = (d_hidden * gelu_slope(pre)).astype(BF16).astype(F32)
    hidden = gelu_value(pre).astype(BF16)
    pairs = lax.dot_general(hidden, cot, (((1,), (1,)), ((), ())), preferred_element_type=F32)
    spans = jnp.dot(pairs, column_ref[...], precision=HIGHEST, preferred_element_type=F32)
    depth = lax.broadcasted_iota(jnp.int32, (ROWS, 128), 0) // OWN
    kept = jnp.zeros((ROWS, 128), F32)
    for z in range(SIZE_Z):
        kept = jnp.where(depth == z + 1, spans[:, 128 * z : 128 * z + 128], kept)
    head = jnp.dot(row_ref[...], kept, precision=HIGHEST, preferred_element_type=F32)

    stack_moved([d_pre[:, 128 * at : 128 * at + 128] for at in range(BLOCKS)], stack_s)
    back = stack_s[...].astype(BF16)
    total = jnp.zeros((256, 256), F32)
    for pair in range(2):
        taps = jnp.dot(tap_ref[pair], back, preferred_element_type=F32).astype(BF16)
        total = total + jnp.dot(taps, in_s[pair], preferred_element_type=F32)
    up = total[0:128, 0:128] + total[128:256, 0:128]
    skip = total[0:128, 128:256] + rolled(total[128:256, 128:256], 64)
    half = low_half((32, 128))
    for even in range(0, OWN, 2):
        first, second = slice(32 * even, 32 * even + 32), slice(32 * even + 32, 32 * even + 64)
        turned = rolled(up[second], 64)
        start = 192 * even
        share_ref[:, start : start + 128] = up[first] + head if even == 0 else up[first]
        share_ref[:, start + 128 : start + 256] = jnp.where(half, skip[first], turned)
        share_ref[:, start + 256 : start + 384] = jnp.where(half, turned, rolled(skip[second], 64))


def input_kernel(field_ref, head_ref, weight_ref, skip_ref, coarse_ref, cot_s, pre_s, window_s, sum_s):
    cot_s[:, 0:8, :] = jnp.zeros((12, 8, 128), F32)
    cot_s[:, 8:40, :] = field_ref[:, :, 384:512].astype(F32)
    total = jnp.zeros((240, 384), F32)
    for a in (-1, 0, 1):
        for b in (-1, 0, 1):
            moved = cot_s[1 - a : 11 - a, 8 - b : 32 - b, :].reshape(240, 128).astype(BF16)
            total = total + jnp.dot(
                moved[:, :32], head_ref[3 * (a + 1) + b + 1], preferred_element_type=F32
            )
    pre_wide = field_ref[1:11, :, 0:384].astype(F32)[:, :24].reshape(240, 384)
    d_pre = (total * gelu_slope(pre_wide)).astype(BF16).astype(F32)
    pre_s[...] = d_pre.reshape(10, 24, 384)

    half = low_half((10, 16, 128))
    for b in (-1, 0, 1):
        moved = pre_s[:, 2 - b : 18 - b, :]
        shifted = rolled(moved, 320)
        for z in range(SIZE_Z):
            source, start = (moved, 64 * z) if z % 2 == 0 else (shifted, 64 * z - 64)
            low = source[:, :, start : start + 128]
            high = jnp.where(half, source[:, :, start + 128 : start + 256], 0.0)
            window_s[b + 1, z, :, :, 0:128] = low.astype(BF16)
            window_s[b + 1, z, :, :, 128:256] = high.astype(BF16)

    windows = [
        window_s[b + 1, :, 1 - a : 9 - a].reshape(CELLS, 256)
        for a in (-1, 0, 1)
        for b in (-1, 0, 1)
    ]
    total = jnp.dot(
        jnp.concatenate(windows, axis=1),
        weight_ref[...].reshape(9 * 256, 256),
        preferred_element_type=F32,
    ).reshape(SIZE_Z, SIZE_X, SIZE_Y, 256)
    half = low_half((8, 16, 128))
    for pair in range(2):
        even, odd = total[2 * pair], total[2 * pair + 1]
        lanes = slice(128 * pair, 128 * pair + 128)
        skip_ref[:, :, lanes] = jnp.where(half, even[..., 128:], odd[..., 128:]).astype(BF16)
        both = (even[..., :128] + odd[..., :128]).reshape(4, 2, 16, 128)
        sum_s[...] = (both[:, 0] + both[:, 1]).reshape(64, 128)
        summed = sum_s[pl.ds(0, 32, stride=2), :] + sum_s[pl.ds(1, 32, stride=2), :]
        coarse_ref[:, lanes] = summed.astype(BF16)


def traded(parts, axes):
    return lax.all_to_all(parts, axes, 0, 0)


def spread(part, axes):
    peers = lax.axis_size(axes)
    return traded(jnp.broadcast_to(part[None], (peers, *part.shape)), axes)


def per_device(coarse, skip_features, pre_act, cotangent, weight_one, weight_out):
    inputs = plane_inputs(coarse, skip_features)
    head = head_matrix(weight_out)
    deep = depth_rims(pre_act, cotangent)
    share_choice, field_choice = row_choices()
    parts = pl.pallas_call(
        parts_kernel, out_shape=jax.ShapeDtypeStruct((BLOCKS, 48, 128), BF16)
    )(*deep, share_choice)
    parts, inputs = lax.optimization_barrier((parts, inputs))
    data = traded(parts, PLANE)
    share = pl.pallas_call(
        share_kernel,
        out_shape=jax.ShapeDtypeStruct(SHARE, F32),
        scratch_shapes=[
            pltpu.VMEM((216, 2048), F32),
            pltpu.VMEM((2, 2048, 256), BF16),
        ],
        compiler_params=pltpu.CompilerParams(vmem_limit_bytes=40 * 2**20),
        cost_estimate=pl.CostEstimate(
            flops=1_500_000_000, bytes_accessed=2_000_000, transcendentals=200_000
        ),
    )(data, inputs, own_head_matrix(head), *choices())
    deep, share = lax.optimization_barrier((deep, share))
    field = pl.pallas_call(
        field_kernel, out_shape=jax.ShapeDtypeStruct((SIZE_X, SIZE_Y, 512), BF16)
    )(*deep, field_choice)
    field = with_x_rims(field)
    near = jnp.sum(traded(share.reshape(4, 8, SHARE[1]), NEAR), axis=0)
    field, near = lax.optimization_barrier((field, near))
    field = with_y_rims(field)
    far = jnp.sum(spread(near.astype(BF16), FAR).astype(F32), axis=0)
    column = spread(far.astype(BF16), NEAR).reshape(SHARE)
    field, column = lax.optimization_barrier((field, column))
    body, head_grad = pl.pallas_call(
        unpack_kernel,
        out_shape=(
            jax.ShapeDtypeStruct((27, C_HID * 192), F32),
            jax.ShapeDtypeStruct((27, C_VEL, C_HID), F32),
        ),
        compiler_params=pltpu.CompilerParams(vmem_limit_bytes=16 * 2**20),
    )(spread(column, PLANE), head_channels())
    skip_grad, coarse_grad = pl.pallas_call(
        input_kernel,
        out_shape=(
            jax.ShapeDtypeStruct((SIZE_X, SIZE_Y, 256), BF16),
            jax.ShapeDtypeStruct((32, 256), BF16),
        ),
        scratch_shapes=[
            pltpu.VMEM((12, 40, 128), F32),
            pltpu.VMEM((10, 24, 384), F32),
            pltpu.VMEM((3, SIZE_Z, 10, 16, 256), BF16),
            pltpu.VMEM((64, 128), F32),
        ],
        compiler_params=pltpu.CompilerParams(vmem_limit_bytes=32 * 2**20),
        cost_estimate=pl.CostEstimate(
            flops=700_000_000, bytes_accessed=3_000_000, transcendentals=100_000
        ),
    )(field, head, input_matrix(weight_one))
    return coarse_grad.reshape(4, 8, 256), skip_grad, body, head_grad


def solution(mesh):
    names = ("gx", "gy", "gzh", "gzm", "gzl")
    split = Mesh(mesh.devices.reshape(4, 4, 2, 8, 2), names)
    field = P("gx", "gy", GZ)
    return jax.shard_map(
        per_device,
        mesh=split,
        in_specs=(field, field, field, P(None, "gx", "gy", GZ), P(), P()),
        out_specs=(field, field, P(), P()),
        check_vma=False,
    )
```

```python
import jax
import jax.numpy as jnp
import numpy as np
from jax import lax
from jax.experimental import pallas as pl
from jax.experimental.pallas import tpu as pltpu
from jax.sharding import Mesh, PartitionSpec as P

C_UP = 128
C_HID = 64
C_VEL = 3
SIZE_X, SIZE_Y, SIZE_Z = 8, 16, 4
CELLS = SIZE_X * SIZE_Y * SIZE_Z
NORM = 1.0 / 512.0
F32, BF16 = jnp.float32, jnp.bfloat16

GX, GY, GZ = "gx", "gy", ("gzh", "gzm", "gzl")
PLANE = ("gx", "gy")
NEAR = ("gzh", "gzl")
FAR = "gzm"
BLOCKS = 16
OWN = C_HID // BLOCKS
ROWS = 6 * OWN
SHARE = (32, OWN * 192)
HIGHEST = lax.Precision.HIGHEST


root_half = 0.7071067811865476
inv_root_tau = 0.3989422804014327


def gelu_value(values):
    return 0.5 * values * (1.0 + lax.erf(values * root_half))


def gelu_slope(values):
    return (
        0.5 * (1.0 + lax.erf(values * root_half))
        + values * jnp.exp(-0.5 * values * values) * inv_root_tau
    )


def from_both(to_next, to_previous, axis):
    peers = lax.axis_size(axis)
    up = [(i, (i + 1) % peers) for i in range(peers)]
    down = [(j, i) for i, j in up]
    return lax.ppermute(to_next, axis, up), lax.ppermute(to_previous, axis, down)


def depth_rims(pre_act, cotangent):
    cot = jnp.transpose(cotangent, (3, 0, 1, 2)).reshape(SIZE_Z * C_VEL, 128)
    cot = jnp.pad(cot, ((0, 4), (0, 0)))
    rows, high, low = pl.pallas_call(
        turn_kernel,
        out_shape=(
            jax.ShapeDtypeStruct((272, 128), BF16),
            jax.ShapeDtypeStruct((80, 128), BF16),
            jax.ShapeDtypeStruct((80, 128), BF16),
        ),
    )(pre_act.reshape(128, SIZE_Z * C_HID), cot)
    before, after = from_both(high, low, GZ)
    return before, rows, after


def plane_inputs(coarse, skip_features):
    parts = pl.pallas_call(
        message_kernel, out_shape=jax.ShapeDtypeStruct((BLOCKS, 160, 256), BF16)
    )(coarse.reshape(32, 256), skip_features.reshape(128, 256))
    return traded(parts, PLANE)


def with_x_rims(field):
    before, after = from_both(field[6:], field[:2], GX)
    return jnp.concatenate([before, field, after], axis=0)


def with_y_rims(field):
    before, after = from_both(field[:, 14:], field[:, :2], GY)
    fill = jnp.zeros((SIZE_X + 4, 12, 512), BF16)
    return jnp.concatenate([before, field, after, fill], axis=1)


def head_matrix(weight_out):
    taps = weight_out.reshape(9, 3, C_VEL, C_HID)[:, ::-1].reshape(9, 9, C_HID)
    columns = [jnp.pad(taps, ((0, 0), (3 * z, 23 - 3 * z), (0, 0))) for z in range(6)]
    return jnp.concatenate(columns, axis=2)


def own_head_matrix(head):
    place = lax.axis_index(GX) * lax.axis_size(GY) + lax.axis_index(GY)
    split = head[:, :24].reshape(9, 24, 6, BLOCKS, OWN)
    own = lax.dynamic_index_in_dim(split, place, 3, keepdims=False)
    return jnp.transpose(own, (2, 3, 0, 1)).reshape(ROWS, 216)


def row_choices():
    pre_at = lambda z, c: c if z < 0 else 352 + c if z > 3 else 80 + 64 * z + c
    cot_at = lambda z, o: 76 + 3 * z + o if z < 0 else 404 + 3 * z + o if z > 3 else 336 + 3 * z + o
    shares = np.zeros((BLOCKS, 48, 432), np.float32)
    lanes = np.zeros((432, 512), np.float32)
    for z in range(-1, 5):
        for c in range(C_HID):
            shares[c // OWN, OWN * (z + 1) + c % OWN, pre_at(z, c)] = 1.0
            lanes[pre_at(z, c), C_HID * (z + 1) + c] = 1.0
    for z in range(-2, 6):
        for o in range(C_VEL):
            shares[:, ROWS + C_VEL * (z + 2) + o, cot_at(z, o)] = 1.0
            lanes[cot_at(z, o), 384 + C_VEL * (z + 2) + o] = 1.0
    return jnp.asarray(shares.reshape(768, 432), BF16), jnp.asarray(lanes, BF16)


def choices():
    tap_rows = np.zeros((2, 2, OWN, 32, 216), np.float32)
    head_columns = np.zeros((9, 8, C_VEL, SIZE_Z, 128), np.float32)
    for tap in range(27):
        pair, c = tap // 3, tap % 3 - 1
        for z in range(SIZE_Z):
            for own in range(OWN):
                row = ROWS * pair + OWN * (z + 1 - c) + own
                tap_rows[z // 2, z % 2, own, tap, row] = 1.0
            for o in range(C_VEL):
                head_columns[pair, z + 2 - c, o, z, 32 * o + tap] = 1.0
    head_rows = np.zeros((32, 6, OWN), np.float32)
    for own in range(OWN):
        head_rows[27 + own, 1:5, own] = 1.0
    double = np.zeros((SIZE_X, SIZE_Y, SIZE_X // 2, SIZE_Y // 2), np.float32)
    for x in range(SIZE_X):
        for y in range(SIZE_Y):
            double[x, y, x // 2, y // 2] = 1.0
    return (
        jnp.asarray(tap_rows.reshape(2, 256, 216)),
        jnp.asarray(head_columns.reshape(216, 512)),
        jnp.asarray(head_rows.reshape(32, ROWS)),
    ), jnp.asarray(double.reshape(128, 32), BF16)


def head_channels():
    rows = np.zeros((BLOCKS, 32, C_HID), np.float32)
    for at in range(BLOCKS):
        for own in range(OWN):
            rows[at, 27 + own, OWN * at + own] = 1.0
    return jnp.asarray(rows.reshape(512, C_HID), BF16)


def turn_kernel(pre_ref, cot_ref, rows_ref, high_ref, low_ref):
    turned = pre_ref[...].astype(F32).T.astype(BF16)
    rows_ref[0:256, :] = turned
    rows_ref[256:272, :] = cot_ref[...]
    high_ref[0:64, :] = turned[192:256]
    high_ref[64:80, :] = cot_ref[...]
    low_ref[0:64, :] = turned[0:64]
    low_ref[64:80, :] = cot_ref[...]


def joined(before_ref, rows_ref, after_ref):
    return jnp.concatenate([before_ref[...], rows_ref[...], after_ref[...]], axis=0)


def parts_kernel(before_ref, rows_ref, after_ref, choice_ref, parts_ref):
    rows = joined(before_ref, rows_ref, after_ref)
    parts = jnp.dot(choice_ref[...], rows, preferred_element_type=F32)
    parts_ref[...] = parts.astype(BF16).reshape(BLOCKS, 48, 128)


def field_kernel(before_ref, rows_ref, after_ref, choice_ref, field_ref):
    turned = joined(before_ref, rows_ref, after_ref).astype(F32).T.astype(BF16)
    field = jnp.dot(turned, choice_ref[...], preferred_element_type=F32)
    field_ref[...] = field.astype(BF16).reshape(SIZE_X, SIZE_Y, 512)


def unpack_kernel(share_ref, choice_ref, body_ref, head_ref):
    for at in range(BLOCKS):
        wide = share_ref[at].astype(F32) * NORM
        body_ref[:, 768 * at : 768 * at + 768] = wide[0:27]
    rows = share_ref[:, :, 0:128].reshape(512, 128)
    head = lax.dot_general(
        rows, choice_ref[...], (((0,), (0,)), ((), ())), preferred_element_type=F32
    )
    for o in range(C_VEL):
        head_ref[:, o, :] = head[32 * o : 32 * o + 27] * NORM


def input_matrix(weight_one):
    taps = weight_one.reshape(9, 3, C_HID, 192)[:, ::-1].reshape(9, 192, 192)
    wide = jnp.concatenate([taps, taps[..., C_UP:]], axis=2)
    return jnp.pad(wide, ((0, 0), (0, 64), (0, 0)))


def low_half(shape):
    return lax.broadcasted_iota(jnp.int32, shape, len(shape) - 1) < 64


def rolled(values, shift):
    flat = values.reshape(-1, values.shape[-1])
    return pltpu.roll(flat, shift, 1).reshape(values.shape)


def moved_y(blocks, b, lane):
    if b == 0:
        return blocks
    out = []
    for at in range(BLOCKS):
        gx, gy = at // 4, at % 4
        there = blocks[4 * gx + (gy - b) % 4]
        edge = lane % 16 == (0 if b == 1 else 15)
        out.append(
            jnp.where(edge, pltpu.roll(there, -15 * b % 128, 1), pltpu.roll(blocks[at], b % 128, 1))
        )
    return out


def moved_x(blocks, a, lane):
    if a == 0:
        return blocks
    turned = [pltpu.roll(block, 16 * a % 128, 1) for block in blocks]
    edge = lane // 16 == (0 if a == 1 else 7)
    return [
        jnp.where(edge, turned[4 * ((at // 4 - a) % 4) + at % 4], turned[at])
        for at in range(BLOCKS)
    ]


def stack_moved(blocks, stack_ref):
    lane = lax.broadcasted_iota(jnp.int32, (ROWS, 128), 1)
    for b in (-1, 0, 1):
        rows = moved_y(blocks, b, lane)
        for a in (-1, 0, 1):
            start = ROWS * (3 * (a + 1) + b + 1)
            for at, block in enumerate(moved_x(rows, a, lane)):
                stack_ref[start : start + ROWS, 128 * at : 128 * at + 128] = block


def message_kernel(coarse_ref, skip_ref, parts_ref):
    for at in range(BLOCKS):
        parts_ref[at, 0:32, :] = coarse_ref[...]
        parts_ref[at, 32:160, :] = skip_ref[...]


def fine_kernel(input_ref, double_ref, fine_ref):
    for at in range(BLOCKS):
        rows = slice(128 * at, 128 * at + 128)
        fine = jnp.dot(double_ref[...], input_ref[at, 0:32, :], preferred_element_type=F32)
        for pair in range(2):
            lanes = slice(128 * pair, 128 * pair + 128)
            fine_ref[pair, rows, 0:128] = fine[:, lanes].astype(BF16)
            fine_ref[pair, rows, 128:256] = input_ref[at, 32:160, lanes]


def share_kernel(data_ref, fine_ref, head_ref, tap_ref, column_ref, row_ref, share_ref, stack_s):
    blocks = [data_ref[at].astype(F32) for at in range(BLOCKS)]
    stack_moved([block[ROWS:48] for block in blocks], stack_s)
    cot = stack_s[...].astype(BF16)
    pre = jnp.concatenate([block[0:ROWS] for block in blocks], axis=1)
    d_hidden = jnp.dot(head_ref[...], cot, preferred_element_type=F32)
    d_pre = (d_hidden * gelu_slope(pre)).astype(BF16).astype(F32)
    hidden = gelu_value(pre).astype(BF16)
    pairs = lax.dot_general(hidden, cot, (((1,), (1,)), ((), ())), preferred_element_type=F32)
    spans = jnp.dot(pairs, column_ref[...], precision=HIGHEST, preferred_element_type=F32)
    depth = lax.broadcasted_iota(jnp.int32, (ROWS, 128), 0) // OWN
    kept = jnp.zeros((ROWS, 128), F32)
    for z in range(SIZE_Z):
        kept = jnp.where(depth == z + 1, spans[:, 128 * z : 128 * z + 128], kept)
    head = jnp.dot(row_ref[...], kept, precision=HIGHEST, preferred_element_type=F32)

    stack_moved([d_pre[:, 128 * at : 128 * at + 128] for at in range(BLOCKS)], stack_s)
    back = stack_s[...].astype(BF16)
    up = jnp.zeros((128, 128), F32)
    skip = jnp.zeros((128, 128), F32)
    for pair in range(2):
        result = jnp.dot(back, fine_ref[pair], preferred_element_type=F32)
        taps = jnp.dot(
            tap_ref[pair], result, precision=HIGHEST, preferred_element_type=F32
        )
        up = up + taps[0:128, 0:128] + taps[128:256, 0:128]
        skip = skip + taps[0:128, 128:256] + rolled(taps[128:256, 128:256], 64)
    half = low_half((32, 128))
    for even in range(0, OWN, 2):
        first, second = slice(32 * even, 32 * even + 32), slice(32 * even + 32, 32 * even + 64)
        turned = rolled(up[second], 64)
        start = 192 * even
        share_ref[:, start : start + 128] = up[first] + head if even == 0 else up[first]
        share_ref[:, start + 128 : start + 256] = jnp.where(half, skip[first], turned)
        share_ref[:, start + 256 : start + 384] = jnp.where(half, turned, rolled(skip[second], 64))


def input_kernel(field_ref, head_ref, weight_ref, skip_ref, coarse_ref, cot_s, pre_s, window_s, sum_s):
    cot_s[:, 0:8, :] = jnp.zeros((12, 8, 128), F32)
    cot_s[:, 8:40, :] = field_ref[:, :, 384:512].astype(F32)
    total = jnp.zeros((240, 384), F32)
    for a in (-1, 0, 1):
        for b in (-1, 0, 1):
            moved = cot_s[1 - a : 11 - a, 8 - b : 32 - b, :].reshape(240, 128).astype(BF16)
            total = total + jnp.dot(
                moved[:, :32], head_ref[3 * (a + 1) + b + 1], preferred_element_type=F32
            )
    pre_wide = field_ref[1:11, :, 0:384].astype(F32)[:, :24].reshape(240, 384)
    d_pre = (total * gelu_slope(pre_wide)).astype(BF16).astype(F32)
    pre_s[...] = d_pre.reshape(10, 24, 384)

    half = low_half((10, 16, 128))
    for b in (-1, 0, 1):
        moved = pre_s[:, 2 - b : 18 - b, :]
        shifted = rolled(moved, 320)
        for z in range(SIZE_Z):
            source, start = (moved, 64 * z) if z % 2 == 0 else (shifted, 64 * z - 64)
            low = source[:, :, start : start + 128]
            high = jnp.where(half, source[:, :, start + 128 : start + 256], 0.0)
            window_s[b + 1, z, :, :, 0:128] = low.astype(BF16)
            window_s[b + 1, z, :, :, 128:256] = high.astype(BF16)

    windows = [
        window_s[b + 1, :, 1 - a : 9 - a].reshape(CELLS, 256)
        for a in (-1, 0, 1)
        for b in (-1, 0, 1)
    ]
    total = jnp.dot(
        jnp.concatenate(windows, axis=1),
        weight_ref[...].reshape(9 * 256, 256),
        preferred_element_type=F32,
    ).reshape(SIZE_Z, SIZE_X, SIZE_Y, 256)
    half = low_half((8, 16, 128))
    for pair in range(2):
        even, odd = total[2 * pair], total[2 * pair + 1]
        lanes = slice(128 * pair, 128 * pair + 128)
        skip_ref[:, :, lanes] = jnp.where(half, even[..., 128:], odd[..., 128:]).astype(BF16)
        both = (even[..., :128] + odd[..., :128]).reshape(4, 2, 16, 128)
        sum_s[...] = (both[:, 0] + both[:, 1]).reshape(64, 128)
        summed = sum_s[pl.ds(0, 32, stride=2), :] + sum_s[pl.ds(1, 32, stride=2), :]
        coarse_ref[:, lanes] = summed.astype(BF16)


def traded(parts, axes):
    return lax.all_to_all(parts, axes, 0, 0)


def spread(part, axes):
    peers = lax.axis_size(axes)
    return traded(jnp.broadcast_to(part[None], (peers, *part.shape)), axes)


def per_device(coarse, skip_features, pre_act, cotangent, weight_one, weight_out):
    inputs = plane_inputs(coarse, skip_features)
    head = head_matrix(weight_out)
    deep = depth_rims(pre_act, cotangent)
    share_choice, field_choice = row_choices()
    parts = pl.pallas_call(
        parts_kernel, out_shape=jax.ShapeDtypeStruct((BLOCKS, 48, 128), BF16)
    )(*deep, share_choice)
    parts, inputs = lax.optimization_barrier((parts, inputs))
    data = traded(parts, PLANE)
    chosen, double = choices()
    fine = pl.pallas_call(
        fine_kernel,
        out_shape=jax.ShapeDtypeStruct((2, 2048, 256), BF16),
        cost_estimate=pl.CostEstimate(
            flops=300_000_000, bytes_accessed=4_000_000, transcendentals=0
        ),
    )(inputs, double)
    field = pl.pallas_call(
        field_kernel,
        out_shape=jax.ShapeDtypeStruct((SIZE_X, SIZE_Y, 512), BF16),
        cost_estimate=pl.CostEstimate(
            flops=60_000_000, bytes_accessed=4_000_000, transcendentals=0
        ),
    )(*deep, field_choice)
    data, fine, field = lax.optimization_barrier((data, fine, field))
    share = pl.pallas_call(
        share_kernel,
        out_shape=jax.ShapeDtypeStruct(SHARE, F32),
        scratch_shapes=[pltpu.VMEM((216, 2048), F32)],
        compiler_params=pltpu.CompilerParams(vmem_limit_bytes=32 * 2**20),
        cost_estimate=pl.CostEstimate(
            flops=1_500_000_000, bytes_accessed=2_000_000, transcendentals=200_000
        ),
    )(data, fine, own_head_matrix(head), *chosen)
    near = jnp.sum(traded(share.reshape(4, 8, SHARE[1]), NEAR), axis=0)
    field, near = lax.optimization_barrier((field, near))
    field = with_x_rims(field)
    far = jnp.sum(spread(near.astype(BF16), FAR).astype(F32), axis=0)
    field, far = lax.optimization_barrier((field, far))
    field = with_y_rims(field)
    column = spread(far.astype(BF16), NEAR).reshape(SHARE)
    field, column = lax.optimization_barrier((field, column))
    body, head_grad = pl.pallas_call(
        unpack_kernel,
        out_shape=(
            jax.ShapeDtypeStruct((27, C_HID * 192), F32),
            jax.ShapeDtypeStruct((27, C_VEL, C_HID), F32),
        ),
        compiler_params=pltpu.CompilerParams(vmem_limit_bytes=16 * 2**20),
    )(spread(column, PLANE), head_channels())
    skip_grad, coarse_grad = pl.pallas_call(
        input_kernel,
        out_shape=(
            jax.ShapeDtypeStruct((SIZE_X, SIZE_Y, 256), BF16),
            jax.ShapeDtypeStruct((32, 256), BF16),
        ),
        scratch_shapes=[
            pltpu.VMEM((12, 40, 128), F32),
            pltpu.VMEM((10, 24, 384), F32),
            pltpu.VMEM((3, SIZE_Z, 10, 16, 256), BF16),
            pltpu.VMEM((64, 128), F32),
        ],
        compiler_params=pltpu.CompilerParams(vmem_limit_bytes=32 * 2**20),
        cost_estimate=pl.CostEstimate(
            flops=700_000_000, bytes_accessed=3_000_000, transcendentals=100_000
        ),
    )(field, head, input_matrix(weight_one))
    return coarse_grad.reshape(4, 8, 256), skip_grad, body, head_grad


def solution(mesh):
    names = ("gx", "gy", "gzh", "gzm", "gzl")
    split = Mesh(mesh.devices.reshape(4, 4, 2, 8, 2), names)
    field = P("gx", "gy", GZ)
    return jax.shard_map(
        per_device,
        mesh=split,
        in_specs=(field, field, field, P(None, "gx", "gy", GZ), P(), P()),
        out_specs=(field, field, P(), P()),
        check_vma=False,
    )
```

```python
import jax
import jax.numpy as jnp
import numpy as np
from jax import lax
from jax.experimental import pallas as pl
from jax.experimental.pallas import tpu as pltpu
from jax.sharding import Mesh, PartitionSpec as P

C_UP = 128
C_HID = 64
C_VEL = 3
SIZE_X, SIZE_Y, SIZE_Z = 8, 16, 4
CELLS = SIZE_X * SIZE_Y * SIZE_Z
NORM = 1.0 / 512.0
F32, BF16 = jnp.float32, jnp.bfloat16

GX, GY, GZ = "gx", "gy", ("gzh", "gzm", "gzl")
PLANE = ("gx", "gy")
NEAR = ("gzh", "gzl")
FAR = "gzm"
BLOCKS = 16
OWN = C_HID // BLOCKS
ROWS = 6 * OWN
SHARE = (32, OWN * 192)
HIGHEST = lax.Precision.HIGHEST


root_half = 0.7071067811865476
inv_root_tau = 0.3989422804014327


def gelu_value(values):
    return 0.5 * values * (1.0 + lax.erf(values * root_half))


def gelu_slope(values):
    return (
        0.5 * (1.0 + lax.erf(values * root_half))
        + values * jnp.exp(-0.5 * values * values) * inv_root_tau
    )


def from_both(to_next, to_previous, axis):
    peers = lax.axis_size(axis)
    up = [(i, (i + 1) % peers) for i in range(peers)]
    down = [(j, i) for i, j in up]
    return lax.ppermute(to_next, axis, up), lax.ppermute(to_previous, axis, down)


def depth_rims(pre_act, cotangent):
    cot = jnp.transpose(cotangent, (3, 0, 1, 2)).reshape(SIZE_Z * C_VEL, 128)
    cot = jnp.pad(cot, ((0, 4), (0, 0)))
    rows, high, low = pl.pallas_call(
        turn_kernel,
        out_shape=(
            jax.ShapeDtypeStruct((272, 128), BF16),
            jax.ShapeDtypeStruct((80, 128), BF16),
            jax.ShapeDtypeStruct((80, 128), BF16),
        ),
    )(pre_act.reshape(128, SIZE_Z * C_HID), cot)
    before, after = from_both(high, low, GZ)
    return before, rows, after


def plane_inputs(coarse, skip_features):
    parts = pl.pallas_call(
        message_kernel, out_shape=jax.ShapeDtypeStruct((BLOCKS, 160, 256), BF16)
    )(coarse.reshape(32, 256), skip_features.reshape(128, 256))
    return traded(parts, PLANE)


def with_x_rims(field):
    before, after = from_both(field[6:], field[:2], GX)
    return jnp.concatenate([before, field, after], axis=0)


def with_y_rims(field):
    before, after = from_both(field[:, 14:], field[:, :2], GY)
    fill = jnp.zeros((SIZE_X + 4, 12, 512), BF16)
    return jnp.concatenate([before, field, after, fill], axis=1)


def head_matrix(weight_out):
    taps = weight_out.reshape(9, 3, C_VEL, C_HID)[:, ::-1].reshape(9, 9, C_HID)
    columns = [jnp.pad(taps, ((0, 0), (3 * z, 23 - 3 * z), (0, 0))) for z in range(6)]
    return jnp.concatenate(columns, axis=2)


def own_head_matrix(head):
    place = lax.axis_index(GX) * lax.axis_size(GY) + lax.axis_index(GY)
    split = head[:, :24].reshape(9, 24, 6, BLOCKS, OWN)
    own = lax.dynamic_index_in_dim(split, place, 3, keepdims=False)
    return jnp.transpose(own, (2, 3, 0, 1)).reshape(ROWS, 216)


def row_choices():
    pre_at = lambda z, c: c if z < 0 else 352 + c if z > 3 else 80 + 64 * z + c
    cot_at = lambda z, o: 76 + 3 * z + o if z < 0 else 404 + 3 * z + o if z > 3 else 336 + 3 * z + o
    shares = np.zeros((BLOCKS, ROWS, 432), np.float32)
    cots = np.zeros((24, 432), np.float32)
    lanes = np.zeros((432, 512), np.float32)
    for z in range(-1, 5):
        for c in range(C_HID):
            shares[c // OWN, OWN * (z + 1) + c % OWN, pre_at(z, c)] = 1.0
            lanes[pre_at(z, c), C_HID * (z + 1) + c] = 1.0
    for z in range(-2, 6):
        for o in range(C_VEL):
            cots[C_VEL * (z + 2) + o, cot_at(z, o)] = 1.0
            lanes[cot_at(z, o), 384 + C_VEL * (z + 2) + o] = 1.0
    rows = np.concatenate([shares.reshape(BLOCKS * ROWS, 432), cots], axis=0)
    return jnp.asarray(rows, BF16), jnp.asarray(lanes, BF16)


def choices():
    tap_rows = np.zeros((2, 2, OWN, 32, 216), np.float32)
    head_columns = np.zeros((9, 8, C_VEL, SIZE_Z, 128), np.float32)
    for tap in range(27):
        pair, c = tap // 3, tap % 3 - 1
        for z in range(SIZE_Z):
            for own in range(OWN):
                row = ROWS * pair + OWN * (z + 1 - c) + own
                tap_rows[z // 2, z % 2, own, tap, row] = 1.0
            for o in range(C_VEL):
                head_columns[pair, z + 2 - c, o, z, 32 * o + tap] = 1.0
    head_rows = np.zeros((32, 6, OWN), np.float32)
    for own in range(OWN):
        head_rows[27 + own, 1:5, own] = 1.0
    double = np.zeros((SIZE_X, SIZE_Y, SIZE_X // 2, SIZE_Y // 2), np.float32)
    for x in range(SIZE_X):
        for y in range(SIZE_Y):
            double[x, y, x // 2, y // 2] = 1.0
    return (
        jnp.asarray(tap_rows.reshape(2, 256, 216), BF16),
        jnp.asarray(head_columns.reshape(216, 512)),
        jnp.asarray(head_rows.reshape(32, ROWS)),
    ), jnp.asarray(double.reshape(128, 32), BF16)


def head_channels():
    rows = np.zeros((BLOCKS, 32, C_HID), np.float32)
    for at in range(BLOCKS):
        for own in range(OWN):
            rows[at, 27 + own, OWN * at + own] = 1.0
    return jnp.asarray(rows.reshape(512, C_HID), BF16)


def turn_kernel(pre_ref, cot_ref, rows_ref, high_ref, low_ref):
    turned = pre_ref[...].astype(F32).T.astype(BF16)
    rows_ref[0:256, :] = turned
    rows_ref[256:272, :] = cot_ref[...]
    high_ref[0:64, :] = turned[192:256]
    high_ref[64:80, :] = cot_ref[...]
    low_ref[0:64, :] = turned[0:64]
    low_ref[64:80, :] = cot_ref[...]


def joined(before_ref, rows_ref, after_ref):
    return jnp.concatenate([before_ref[...], rows_ref[...], after_ref[...]], axis=0)


def parts_kernel(before_ref, rows_ref, after_ref, choice_ref, parts_ref):
    rows = joined(before_ref, rows_ref, after_ref)
    parts = jnp.dot(choice_ref[...], rows, preferred_element_type=F32)
    cot = parts[BLOCKS * ROWS :]
    for at in range(BLOCKS):
        both = jnp.concatenate([parts[ROWS * at : ROWS * at + ROWS], cot], axis=0)
        parts_ref[at] = both.astype(BF16)


def field_kernel(before_ref, rows_ref, after_ref, choice_ref, field_ref):
    turned = joined(before_ref, rows_ref, after_ref).astype(F32).T.astype(BF16)
    field = jnp.dot(turned, choice_ref[...], preferred_element_type=F32)
    field_ref[...] = field.astype(BF16).reshape(SIZE_X, SIZE_Y, 512)


def unpack_kernel(share_ref, choice_ref, body_ref, head_ref):
    for at in range(BLOCKS):
        wide = share_ref[at].astype(F32) * NORM
        body_ref[:, 768 * at : 768 * at + 768] = wide[0:27]
    rows = share_ref[:, :, 0:128].reshape(512, 128)
    head = lax.dot_general(
        rows, choice_ref[...], (((0,), (0,)), ((), ())), preferred_element_type=F32
    )
    for o in range(C_VEL):
        head_ref[:, o, :] = head[32 * o : 32 * o + 27] * NORM


def input_matrix(weight_one):
    taps = weight_one.reshape(9, 3, C_HID, 192)[:, ::-1].reshape(9, 192, 192)
    wide = jnp.concatenate([taps, taps[..., C_UP:]], axis=2)
    return jnp.pad(wide, ((0, 0), (0, 64), (0, 0)))


def low_half(shape):
    return lax.broadcasted_iota(jnp.int32, shape, len(shape) - 1) < 64


def rolled(values, shift):
    flat = values.reshape(-1, values.shape[-1])
    return pltpu.roll(flat, shift, 1).reshape(values.shape)


def moved_y(blocks, b, lane):
    if b == 0:
        return blocks
    out = []
    for at in range(BLOCKS):
        gx, gy = at // 4, at % 4
        there = blocks[4 * gx + (gy - b) % 4]
        edge = lane % 16 == (0 if b == 1 else 15)
        out.append(
            jnp.where(edge, pltpu.roll(there, -15 * b % 128, 1), pltpu.roll(blocks[at], b % 128, 1))
        )
    return out


def moved_x(blocks, a, lane):
    if a == 0:
        return blocks
    turned = [pltpu.roll(block, 16 * a % 128, 1) for block in blocks]
    edge = lane // 16 == (0 if a == 1 else 7)
    return [
        jnp.where(edge, turned[4 * ((at // 4 - a) % 4) + at % 4], turned[at])
        for at in range(BLOCKS)
    ]


def stack_moved(blocks, stack_ref):
    lane = lax.broadcasted_iota(jnp.int32, (ROWS, 128), 1)
    for b in (-1, 0, 1):
        rows = moved_y(blocks, b, lane)
        for a in (-1, 0, 1):
            start = ROWS * (3 * (a + 1) + b + 1)
            for at, block in enumerate(moved_x(rows, a, lane)):
                stack_ref[start : start + ROWS, 128 * at : 128 * at + 128] = block


def message_kernel(coarse_ref, skip_ref, parts_ref):
    for at in range(BLOCKS):
        parts_ref[at, 0:32, :] = coarse_ref[...]
        parts_ref[at, 32:160, :] = skip_ref[...]


def fine_kernel(input_ref, double_ref, fine_ref):
    for at in range(BLOCKS):
        rows = slice(128 * at, 128 * at + 128)
        fine = jnp.dot(double_ref[...], input_ref[at, 0:32, :], preferred_element_type=F32)
        for pair in range(2):
            lanes = slice(128 * pair, 128 * pair + 128)
            fine_ref[pair, rows, 0:128] = fine[:, lanes].astype(BF16)
            fine_ref[pair, rows, 128:256] = input_ref[at, 32:160, lanes]


def share_kernel(data_ref, fine_ref, head_ref, tap_ref, column_ref, row_ref, share_ref, stack_s):
    blocks = [data_ref[at].astype(F32) for at in range(BLOCKS)]
    stack_moved([block[ROWS:48] for block in blocks], stack_s)
    cot = stack_s[...].astype(BF16)
    pre = jnp.concatenate([block[0:ROWS] for block in blocks], axis=1)
    d_hidden = jnp.dot(head_ref[...], cot, preferred_element_type=F32)
    d_pre = (d_hidden * gelu_slope(pre)).astype(BF16).astype(F32)
    hidden = gelu_value(pre).astype(BF16)
    pairs = lax.dot_general(hidden, cot, (((1,), (1,)), ((), ())), preferred_element_type=F32)
    spans = jnp.dot(pairs, column_ref[...], precision=HIGHEST, preferred_element_type=F32)
    depth = lax.broadcasted_iota(jnp.int32, (ROWS, 128), 0) // OWN
    kept = jnp.zeros((ROWS, 128), F32)
    for z in range(SIZE_Z):
        kept = jnp.where(depth == z + 1, spans[:, 128 * z : 128 * z + 128], kept)
    head = jnp.dot(row_ref[...], kept, precision=HIGHEST, preferred_element_type=F32)

    stack_moved([d_pre[:, 128 * at : 128 * at + 128] for at in range(BLOCKS)], stack_s)
    back = stack_s[...].astype(BF16)
    up = jnp.zeros((128, 128), F32)
    skip = jnp.zeros((128, 128), F32)
    for pair in range(2):
        result = jnp.dot(back, fine_ref[pair], preferred_element_type=F32)
        taps = jnp.dot(
            tap_ref[pair].astype(F32), result, precision=HIGHEST, preferred_element_type=F32
        )
        up = up + taps[0:128, 0:128] + taps[128:256, 0:128]
        skip = skip + taps[0:128, 128:256] + rolled(taps[128:256, 128:256], 64)
    half = low_half((32, 128))
    for even in range(0, OWN, 2):
        first, second = slice(32 * even, 32 * even + 32), slice(32 * even + 32, 32 * even + 64)
        turned = rolled(up[second], 64)
        start = 192 * even
        share_ref[:, start : start + 128] = up[first] + head if even == 0 else up[first]
        share_ref[:, start + 128 : start + 256] = jnp.where(half, skip[first], turned)
        share_ref[:, start + 256 : start + 384] = jnp.where(half, turned, rolled(skip[second], 64))


def input_kernel(field_ref, head_ref, weight_ref, skip_ref, coarse_ref, cot_s, pre_s, window_s, sum_s):
    cot_s[:, 0:8, :] = jnp.zeros((12, 8, 128), F32)
    cot_s[:, 8:40, :] = field_ref[:, :, 384:512].astype(F32)
    total = jnp.zeros((240, 384), F32)
    for a in (-1, 0, 1):
        for b in (-1, 0, 1):
            moved = cot_s[1 - a : 11 - a, 8 - b : 32 - b, :].reshape(240, 128).astype(BF16)
            total = total + jnp.dot(
                moved[:, :32], head_ref[3 * (a + 1) + b + 1], preferred_element_type=F32
            )
    pre_wide = field_ref[1:11, :, 0:384].astype(F32)[:, :24].reshape(240, 384)
    d_pre = (total * gelu_slope(pre_wide)).astype(BF16).astype(F32)
    pre_s[...] = d_pre.reshape(10, 24, 384)

    half = low_half((10, 16, 128))
    for b in (-1, 0, 1):
        moved = pre_s[:, 2 - b : 18 - b, :]
        shifted = rolled(moved, 320)
        for z in range(SIZE_Z):
            source, start = (moved, 64 * z) if z % 2 == 0 else (shifted, 64 * z - 64)
            low = source[:, :, start : start + 128]
            high = jnp.where(half, source[:, :, start + 128 : start + 256], 0.0)
            window_s[b + 1, z, :, :, 0:128] = low.astype(BF16)
            window_s[b + 1, z, :, :, 128:256] = high.astype(BF16)

    windows = [
        window_s[b + 1, :, 1 - a : 9 - a].reshape(CELLS, 256)
        for a in (-1, 0, 1)
        for b in (-1, 0, 1)
    ]
    total = jnp.dot(
        jnp.concatenate(windows, axis=1),
        weight_ref[...].reshape(9 * 256, 256),
        preferred_element_type=F32,
    ).reshape(SIZE_Z, SIZE_X, SIZE_Y, 256)
    half = low_half((8, 16, 128))
    for pair in range(2):
        even, odd = total[2 * pair], total[2 * pair + 1]
        lanes = slice(128 * pair, 128 * pair + 128)
        skip_ref[:, :, lanes] = jnp.where(half, even[..., 128:], odd[..., 128:]).astype(BF16)
        both = (even[..., :128] + odd[..., :128]).reshape(4, 2, 16, 128)
        sum_s[...] = (both[:, 0] + both[:, 1]).reshape(64, 128)
        summed = sum_s[pl.ds(0, 32, stride=2), :] + sum_s[pl.ds(1, 32, stride=2), :]
        coarse_ref[:, lanes] = summed.astype(BF16)


def traded(parts, axes):
    return lax.all_to_all(parts, axes, 0, 0)


def spread(part, axes):
    peers = lax.axis_size(axes)
    return traded(jnp.broadcast_to(part[None], (peers, *part.shape)), axes)


def per_device(coarse, skip_features, pre_act, cotangent, weight_one, weight_out):
    inputs = plane_inputs(coarse, skip_features)
    head = head_matrix(weight_out)
    deep = depth_rims(pre_act, cotangent)
    share_choice, field_choice = row_choices()
    parts = pl.pallas_call(
        parts_kernel, out_shape=jax.ShapeDtypeStruct((BLOCKS, 48, 128), BF16)
    )(*deep, share_choice)
    parts, inputs = lax.optimization_barrier((parts, inputs))
    data = traded(parts, PLANE)
    chosen, double = choices()
    fine = pl.pallas_call(
        fine_kernel,
        out_shape=jax.ShapeDtypeStruct((2, 2048, 256), BF16),
        cost_estimate=pl.CostEstimate(
            flops=300_000_000, bytes_accessed=4_000_000, transcendentals=0
        ),
    )(inputs, double)
    field = pl.pallas_call(
        field_kernel,
        out_shape=jax.ShapeDtypeStruct((SIZE_X, SIZE_Y, 512), BF16),
        cost_estimate=pl.CostEstimate(
            flops=60_000_000, bytes_accessed=4_000_000, transcendentals=0
        ),
    )(*deep, field_choice)
    data, fine, field = lax.optimization_barrier((data, fine, field))
    share = pl.pallas_call(
        share_kernel,
        out_shape=jax.ShapeDtypeStruct(SHARE, F32),
        scratch_shapes=[pltpu.VMEM((216, 2048), F32)],
        compiler_params=pltpu.CompilerParams(vmem_limit_bytes=32 * 2**20),
        cost_estimate=pl.CostEstimate(
            flops=1_500_000_000, bytes_accessed=2_000_000, transcendentals=200_000
        ),
    )(data, fine, own_head_matrix(head), *chosen)
    near = jnp.sum(traded(share.reshape(4, 8, SHARE[1]), NEAR), axis=0)
    field, near = lax.optimization_barrier((field, near))
    field = with_x_rims(field)
    far = jnp.sum(spread(near.astype(BF16), FAR).astype(F32), axis=0)
    column = spread(far.astype(BF16), NEAR).reshape(SHARE)
    field, column = lax.optimization_barrier((field, column))
    field = with_y_rims(field)
    body, head_grad = pl.pallas_call(
        unpack_kernel,
        out_shape=(
            jax.ShapeDtypeStruct((27, C_HID * 192), F32),
            jax.ShapeDtypeStruct((27, C_VEL, C_HID), F32),
        ),
        compiler_params=pltpu.CompilerParams(vmem_limit_bytes=16 * 2**20),
    )(spread(column, PLANE), head_channels())
    skip_grad, coarse_grad = pl.pallas_call(
        input_kernel,
        out_shape=(
            jax.ShapeDtypeStruct((SIZE_X, SIZE_Y, 256), BF16),
            jax.ShapeDtypeStruct((32, 256), BF16),
        ),
        scratch_shapes=[
            pltpu.VMEM((12, 40, 128), F32),
            pltpu.VMEM((10, 24, 384), F32),
            pltpu.VMEM((3, SIZE_Z, 10, 16, 256), BF16),
            pltpu.VMEM((64, 128), F32),
        ],
        compiler_params=pltpu.CompilerParams(vmem_limit_bytes=32 * 2**20),
        cost_estimate=pl.CostEstimate(
            flops=700_000_000, bytes_accessed=3_000_000, transcendentals=100_000
        ),
    )(field, head, input_matrix(weight_one))
    return coarse_grad.reshape(4, 8, 256), skip_grad, body, head_grad


def solution(mesh):
    names = ("gx", "gy", "gzh", "gzm", "gzl")
    split = Mesh(mesh.devices.reshape(4, 4, 2, 8, 2), names)
    field = P("gx", "gy", GZ)
    return jax.shard_map(
        per_device,
        mesh=split,
        in_specs=(field, field, field, P(None, "gx", "gy", GZ), P(), P()),
        out_specs=(field, field, P(), P()),
        check_vma=False,
    )
```

```python
import jax
import jax.numpy as jnp
import numpy as np
from jax import lax
from jax.experimental import pallas as pl
from jax.experimental.pallas import tpu as pltpu
from jax.sharding import Mesh, PartitionSpec as P

C_UP = 128
C_HID = 64
C_VEL = 3
SIZE_X, SIZE_Y, SIZE_Z = 8, 16, 4
CELLS = SIZE_X * SIZE_Y * SIZE_Z
NORM = 1.0 / 512.0
F32, BF16 = jnp.float32, jnp.bfloat16

GX, GY, GZ = "gx", "gy", ("gzh", "gzm", "gzl")
PLANE = ("gx", "gy")
NEAR = ("gzh", "gzl")
FAR = "gzm"
BLOCKS = 16
OWN = C_HID // BLOCKS
ROWS = 6 * OWN
SHARE = (32, OWN * 192)
HIGHEST = lax.Precision.HIGHEST


root_half = 0.7071067811865476
inv_root_tau = 0.3989422804014327


def gelu_value(values):
    return 0.5 * values * (1.0 + lax.erf(values * root_half))


def gelu_slope(values):
    return (
        0.5 * (1.0 + lax.erf(values * root_half))
        + values * jnp.exp(-0.5 * values * values) * inv_root_tau
    )


def from_both(to_next, to_previous, axis):
    peers = lax.axis_size(axis)
    up = [(i, (i + 1) % peers) for i in range(peers)]
    down = [(j, i) for i, j in up]
    return lax.ppermute(to_next, axis, up), lax.ppermute(to_previous, axis, down)


def depth_rims(pre_act, cotangent):
    cot = jnp.transpose(cotangent, (3, 0, 1, 2)).reshape(SIZE_Z * C_VEL, 128)
    cot = jnp.pad(cot, ((0, 4), (0, 0)))
    rows, high, low = pl.pallas_call(
        turn_kernel,
        out_shape=(
            jax.ShapeDtypeStruct((272, 128), BF16),
            jax.ShapeDtypeStruct((80, 128), BF16),
            jax.ShapeDtypeStruct((80, 128), BF16),
        ),
    )(pre_act.reshape(128, SIZE_Z * C_HID), cot)
    before, after = from_both(high, low, GZ)
    return before, rows, after


def plane_inputs(coarse, skip_features):
    parts = pl.pallas_call(
        message_kernel,
        out_shape=jax.ShapeDtypeStruct((BLOCKS, 160, 256), BF16),
        out_specs=pl.BlockSpec(memory_space=pl.ANY),
        scratch_shapes=[pltpu.SemaphoreType.DMA((2, BLOCKS))],
    )(coarse.reshape(32, 256), skip_features.reshape(128, 256))
    return traded(parts, PLANE)


def with_x_rims(field):
    before, after = from_both(field[6:], field[:2], GX)
    return jnp.concatenate([before, field, after], axis=0)


def with_y_rims(field):
    before, after = from_both(field[:, 14:], field[:, :2], GY)
    fill = jnp.zeros((SIZE_X + 4, 12, 512), BF16)
    return jnp.concatenate([before, field, after, fill], axis=1)


def head_matrix(weight_out):
    taps = weight_out.reshape(9, 3, C_VEL, C_HID)[:, ::-1].reshape(9, 9, C_HID)
    columns = [jnp.pad(taps, ((0, 0), (3 * z, 23 - 3 * z), (0, 0))) for z in range(6)]
    return jnp.concatenate(columns, axis=2)


def own_head_matrix(head):
    place = lax.axis_index(GX) * lax.axis_size(GY) + lax.axis_index(GY)
    split = head[:, :24].reshape(9, 24, 6, BLOCKS, OWN)
    own = lax.dynamic_index_in_dim(split, place, 3, keepdims=False)
    return jnp.transpose(own, (2, 3, 0, 1)).reshape(ROWS, 216)


def row_choices():
    shares = np.zeros((BLOCKS, 6, OWN, 384), np.float32)
    cots = np.zeros((128, 48), np.float32)
    for z in range(6):
        for c in range(C_HID):
            shares[c // OWN, z, c % OWN, C_HID * z + c] = 1.0
    for z in range(-2, 6):
        start = 12 + 3 * z if z < 0 else 20 + 3 * z if z > 3 else 16 + 3 * z
        for o in range(C_VEL):
            cots[C_VEL * (z + 2) + o, start + o] = 1.0
    return jnp.asarray(shares.reshape(384, 384), BF16), jnp.asarray(cots, BF16)


def choices():
    tap_rows = np.zeros((2, 2, OWN, 32, 216), np.float32)
    head_columns = np.zeros((9, 8, C_VEL, SIZE_Z, 128), np.float32)
    for tap in range(27):
        pair, c = tap // 3, tap % 3 - 1
        for z in range(SIZE_Z):
            for own in range(OWN):
                row = ROWS * pair + OWN * (z + 1 - c) + own
                tap_rows[z // 2, z % 2, own, tap, row] = 1.0
            for o in range(C_VEL):
                head_columns[pair, z + 2 - c, o, z, 32 * o + tap] = 1.0
    head_rows = np.zeros((32, 6, OWN), np.float32)
    for own in range(OWN):
        head_rows[27 + own, 1:5, own] = 1.0
    double = np.zeros((SIZE_X, SIZE_Y, SIZE_X // 2, SIZE_Y // 2), np.float32)
    for x in range(SIZE_X):
        for y in range(SIZE_Y):
            double[x, y, x // 2, y // 2] = 1.0
    return (
        jnp.asarray(tap_rows.reshape(2, 256, 216), BF16),
        jnp.asarray(head_columns.reshape(216, 512), BF16),
        jnp.asarray(head_rows.reshape(32, ROWS)),
    ), jnp.asarray(double.reshape(128, 32), BF16)


def head_channels():
    rows = np.zeros((BLOCKS, 32, C_HID), np.float32)
    for at in range(BLOCKS):
        for own in range(OWN):
            rows[at, 27 + own, OWN * at + own] = 1.0
    return jnp.asarray(rows.reshape(512, C_HID), BF16)


def turn_kernel(pre_ref, cot_ref, rows_ref, high_ref, low_ref):
    turned = pre_ref[...].astype(F32).T.astype(BF16)
    rows_ref[0:256, :] = turned
    rows_ref[256:272, :] = cot_ref[...]
    high_ref[0:64, :] = turned[192:256]
    high_ref[64:80, :] = cot_ref[...]
    low_ref[0:64, :] = turned[0:64]
    low_ref[64:80, :] = cot_ref[...]


def joined(before_ref, rows_ref, after_ref, cot_choice_ref):
    pre = jnp.concatenate([before_ref[0:64, :], rows_ref[0:256, :], after_ref[0:64, :]], axis=0)
    cot = jnp.concatenate(
        [before_ref[64:80, :], rows_ref[256:272, :], after_ref[64:80, :]], axis=0
    )
    return pre, jnp.dot(cot_choice_ref[...], cot, preferred_element_type=F32)


def parts_kernel(before_ref, rows_ref, after_ref, choice_ref, cot_choice_ref, parts_ref):
    pre, cot = joined(before_ref, rows_ref, after_ref, cot_choice_ref)
    parts = jnp.dot(choice_ref[...], pre, preferred_element_type=F32)
    for at in range(BLOCKS):
        both = jnp.concatenate([parts[ROWS * at : ROWS * at + ROWS], cot[0:24]], axis=0)
        parts_ref[at] = both.astype(BF16)


def field_kernel(before_ref, rows_ref, after_ref, cot_choice_ref, field_ref):
    pre, cot = joined(before_ref, rows_ref, after_ref, cot_choice_ref)
    field = jnp.concatenate([pre.astype(F32), cot], axis=0).T
    field_ref[...] = field.astype(BF16).reshape(SIZE_X, SIZE_Y, 512)


def unpack_kernel(share_ref, choice_ref, body_ref, head_ref):
    for at in range(BLOCKS):
        wide = share_ref[at].astype(F32) * NORM
        body_ref[:, 768 * at : 768 * at + 768] = wide[0:27]
    rows = share_ref[:, :, 0:128].reshape(512, 128)
    head = lax.dot_general(
        rows, choice_ref[...], (((0,), (0,)), ((), ())), preferred_element_type=F32
    )
    for o in range(C_VEL):
        head_ref[o] = head[32 * o : 32 * o + 27] * NORM


def input_matrix(weight_one):
    taps = weight_one.reshape(9, 3, C_HID, 192)[:, ::-1].reshape(9, 192, 192)
    wide = jnp.concatenate([taps, taps[..., C_UP:]], axis=2)
    return jnp.pad(wide, ((0, 0), (0, 64), (0, 0)))


def low_half(shape):
    return lax.broadcasted_iota(jnp.int32, shape, len(shape) - 1) < 64


def rolled(values, shift):
    flat = values.reshape(-1, values.shape[-1])
    return pltpu.roll(flat, shift, 1).reshape(values.shape)


def moved_y(blocks, b, lane):
    if b == 0:
        return blocks
    out = []
    for at in range(BLOCKS):
        gx, gy = at // 4, at % 4
        there = blocks[4 * gx + (gy - b) % 4]
        edge = lane % 16 == (0 if b == 1 else 15)
        out.append(
            jnp.where(edge, pltpu.roll(there, -15 * b % 128, 1), pltpu.roll(blocks[at], b % 128, 1))
        )
    return out


def moved_x(blocks, a, lane):
    if a == 0:
        return blocks
    turned = [pltpu.roll(block, 16 * a % 128, 1) for block in blocks]
    edge = lane // 16 == (0 if a == 1 else 7)
    return [
        jnp.where(edge, turned[4 * ((at // 4 - a) % 4) + at % 4], turned[at])
        for at in range(BLOCKS)
    ]


def stack_moved(blocks, stack_ref):
    lane = lax.broadcasted_iota(jnp.int32, (ROWS, 128), 1)
    for b in (-1, 0, 1):
        rows = moved_y(blocks, b, lane)
        for a in (-1, 0, 1):
            start = ROWS * (3 * (a + 1) + b + 1)
            for at, block in enumerate(moved_x(rows, a, lane)):
                stack_ref[start : start + ROWS, 128 * at : 128 * at + 128] = block


def message_kernel(coarse_ref, skip_ref, parts_ref, sems):
    copies = []
    for at in range(BLOCKS):
        copies.append(
            pltpu.make_async_copy(coarse_ref, parts_ref.at[at, 0:32, :], sems.at[0, at])
        )
        copies.append(
            pltpu.make_async_copy(skip_ref, parts_ref.at[at, 32:160, :], sems.at[1, at])
        )
    for copy in copies:
        copy.start()
    for copy in copies:
        copy.wait()


def fine_kernel(input_ref, double_ref, fine_ref):
    for at in range(BLOCKS):
        rows = slice(128 * at, 128 * at + 128)
        fine = jnp.dot(double_ref[...], input_ref[at, 0:32, :], preferred_element_type=F32)
        for pair in range(2):
            lanes = slice(128 * pair, 128 * pair + 128)
            fine_ref[pair, rows, 0:128] = fine[:, lanes].astype(BF16)
            fine_ref[pair, rows, 128:256] = input_ref[at, 32:160, lanes]


def share_kernel(data_ref, fine_ref, head_ref, tap_ref, column_ref, row_ref, share_ref, stack_s):
    blocks = [data_ref[at].astype(F32) for at in range(BLOCKS)]
    stack_moved([block[ROWS:48] for block in blocks], stack_s)
    cot = stack_s[...].astype(BF16)
    pre = jnp.concatenate([block[0:ROWS] for block in blocks], axis=1)
    d_hidden = jnp.dot(head_ref[...], cot, preferred_element_type=F32)
    d_pre = (d_hidden * gelu_slope(pre)).astype(BF16).astype(F32)
    hidden = gelu_value(pre).astype(BF16)
    pairs = lax.dot_general(hidden, cot, (((1,), (1,)), ((), ())), preferred_element_type=F32)
    spans = jnp.dot(
        pairs, column_ref[...].astype(F32), precision=HIGHEST, preferred_element_type=F32
    )
    depth = lax.broadcasted_iota(jnp.int32, (ROWS, 128), 0) // OWN
    kept = jnp.zeros((ROWS, 128), F32)
    for z in range(SIZE_Z):
        kept = jnp.where(depth == z + 1, spans[:, 128 * z : 128 * z + 128], kept)
    head = jnp.dot(row_ref[...], kept, precision=HIGHEST, preferred_element_type=F32)

    stack_moved([d_pre[:, 128 * at : 128 * at + 128] for at in range(BLOCKS)], stack_s)
    back = stack_s[...].astype(BF16)
    up = jnp.zeros((128, 128), F32)
    skip = jnp.zeros((128, 128), F32)
    for pair in range(2):
        result = jnp.dot(back, fine_ref[pair], preferred_element_type=F32)
        taps = jnp.dot(
            tap_ref[pair].astype(F32), result, precision=HIGHEST, preferred_element_type=F32
        )
        up = up + taps[0:128, 0:128] + taps[128:256, 0:128]
        skip = skip + taps[0:128, 128:256] + rolled(taps[128:256, 128:256], 64)
    half = low_half((32, 128))
    for even in range(0, OWN, 2):
        first, second = slice(32 * even, 32 * even + 32), slice(32 * even + 32, 32 * even + 64)
        turned = rolled(up[second], 64)
        start = 192 * even
        share_ref[:, start : start + 128] = up[first] + head if even == 0 else up[first]
        share_ref[:, start + 128 : start + 256] = jnp.where(half, skip[first], turned)
        share_ref[:, start + 256 : start + 384] = jnp.where(half, turned, rolled(skip[second], 64))


def input_kernel(field_ref, head_ref, weight_ref, skip_ref, coarse_ref, cot_s, pre_s, window_s, sum_s):
    cot_s[:, 0:8, :] = jnp.zeros((12, 8, 128), F32)
    cot_s[:, 8:40, :] = field_ref[:, :, 384:512].astype(F32)
    total = jnp.zeros((240, 384), F32)
    for a in (-1, 0, 1):
        for b in (-1, 0, 1):
            moved = cot_s[1 - a : 11 - a, 8 - b : 32 - b, :].reshape(240, 128).astype(BF16)
            total = total + jnp.dot(
                moved[:, :32], head_ref[3 * (a + 1) + b + 1], preferred_element_type=F32
            )
    pre_wide = field_ref[1:11, :, 0:384].astype(F32)[:, :24].reshape(240, 384)
    d_pre = (total * gelu_slope(pre_wide)).astype(BF16).astype(F32)
    pre_s[...] = d_pre.reshape(10, 24, 384)

    half = low_half((10, 16, 128))
    for b in (-1, 0, 1):
        moved = pre_s[:, 2 - b : 18 - b, :]
        shifted = rolled(moved, 320)
        for z in range(SIZE_Z):
            source, start = (moved, 64 * z) if z % 2 == 0 else (shifted, 64 * z - 64)
            low = source[:, :, start : start + 128]
            high = jnp.where(half, source[:, :, start + 128 : start + 256], 0.0)
            window_s[b + 1, z, :, :, 0:128] = low.astype(BF16)
            window_s[b + 1, z, :, :, 128:256] = high.astype(BF16)

    windows = [
        window_s[b + 1, :, 1 - a : 9 - a].reshape(CELLS, 256)
        for a in (-1, 0, 1)
        for b in (-1, 0, 1)
    ]
    total = jnp.dot(
        jnp.concatenate(windows, axis=1),
        weight_ref[...].reshape(9 * 256, 256),
        preferred_element_type=F32,
    ).reshape(SIZE_Z, SIZE_X, SIZE_Y, 256)
    half = low_half((8, 16, 128))
    for pair in range(2):
        even, odd = total[2 * pair], total[2 * pair + 1]
        lanes = slice(128 * pair, 128 * pair + 128)
        skip_ref[:, :, lanes] = jnp.where(half, even[..., 128:], odd[..., 128:]).astype(BF16)
        both = (even[..., :128] + odd[..., :128]).reshape(4, 2, 16, 128)
        sum_s[...] = (both[:, 0] + both[:, 1]).reshape(64, 128)
        summed = sum_s[pl.ds(0, 32, stride=2), :] + sum_s[pl.ds(1, 32, stride=2), :]
        coarse_ref[:, lanes] = summed.astype(BF16)


def traded(parts, axes):
    return lax.all_to_all(parts, axes, 0, 0)


def spread(part, axes):
    peers = lax.axis_size(axes)
    return traded(jnp.broadcast_to(part[None], (peers, *part.shape)), axes)


def per_device(coarse, skip_features, pre_act, cotangent, weight_one, weight_out):
    inputs = plane_inputs(coarse, skip_features)
    head = head_matrix(weight_out)
    deep = depth_rims(pre_act, cotangent)
    share_choice, cot_choice = row_choices()
    parts = pl.pallas_call(
        parts_kernel, out_shape=jax.ShapeDtypeStruct((BLOCKS, 48, 128), BF16)
    )(*deep, share_choice, cot_choice)
    parts, inputs = lax.optimization_barrier((parts, inputs))
    data = traded(parts, PLANE)
    chosen, double = choices()
    fine = pl.pallas_call(
        fine_kernel,
        out_shape=jax.ShapeDtypeStruct((2, 2048, 256), BF16),
        cost_estimate=pl.CostEstimate(
            flops=300_000_000, bytes_accessed=4_000_000, transcendentals=0
        ),
    )(inputs, double)
    field = pl.pallas_call(
        field_kernel,
        out_shape=jax.ShapeDtypeStruct((SIZE_X, SIZE_Y, 512), BF16),
        cost_estimate=pl.CostEstimate(
            flops=60_000_000, bytes_accessed=4_000_000, transcendentals=0
        ),
    )(*deep, cot_choice)
    data, fine, field = lax.optimization_barrier((data, fine, field))
    share = pl.pallas_call(
        share_kernel,
        out_shape=jax.ShapeDtypeStruct(SHARE, F32),
        scratch_shapes=[pltpu.VMEM((216, 2048), F32)],
        compiler_params=pltpu.CompilerParams(vmem_limit_bytes=32 * 2**20),
        cost_estimate=pl.CostEstimate(
            flops=1_500_000_000, bytes_accessed=2_000_000, transcendentals=200_000
        ),
    )(data, fine, own_head_matrix(head), *chosen)
    near = jnp.sum(traded(share.reshape(4, 8, SHARE[1]), NEAR), axis=0)
    field, near = lax.optimization_barrier((field, near))
    field = with_y_rims(with_x_rims(field))
    far = jnp.sum(spread(near.astype(BF16), FAR).astype(F32), axis=0)
    field, far = lax.optimization_barrier((field, far))
    column = spread(far.astype(BF16), NEAR).reshape(SHARE)
    field, column = lax.optimization_barrier((field, column))
    body, head_grad = pl.pallas_call(
        unpack_kernel,
        out_shape=(
            jax.ShapeDtypeStruct((27, C_HID * 192), F32),
            jax.ShapeDtypeStruct((C_VEL, 27, C_HID), F32),
        ),
        compiler_params=pltpu.CompilerParams(vmem_limit_bytes=16 * 2**20),
    )(spread(column, PLANE), head_channels())
    skip_grad, coarse_grad = pl.pallas_call(
        input_kernel,
        out_shape=(
            jax.ShapeDtypeStruct((SIZE_X, SIZE_Y, 256), BF16),
            jax.ShapeDtypeStruct((32, 256), BF16),
        ),
        scratch_shapes=[
            pltpu.VMEM((12, 40, 128), F32),
            pltpu.VMEM((10, 24, 384), F32),
            pltpu.VMEM((3, SIZE_Z, 10, 16, 256), BF16),
            pltpu.VMEM((64, 128), F32),
        ],
        compiler_params=pltpu.CompilerParams(vmem_limit_bytes=32 * 2**20),
        cost_estimate=pl.CostEstimate(
            flops=700_000_000, bytes_accessed=3_000_000, transcendentals=100_000
        ),
    )(field, head, input_matrix(weight_one))
    return coarse_grad.reshape(4, 8, 256), skip_grad, body, jnp.transpose(head_grad, (1, 0, 2))


def solution(mesh):
    names = ("gx", "gy", "gzh", "gzm", "gzl")
    split = Mesh(mesh.devices.reshape(4, 4, 2, 8, 2), names)
    field = P("gx", "gy", GZ)
    return jax.shard_map(
        per_device,
        mesh=split,
        in_specs=(field, field, field, P(None, "gx", "gy", GZ), P(), P()),
        out_specs=(field, field, P(), P()),
        check_vma=False,
    )
```

```python
import jax
import jax.numpy as jnp
import numpy as np
from jax import lax
from jax.experimental import pallas as pl
from jax.experimental.pallas import tpu as pltpu
from jax.sharding import Mesh, PartitionSpec as P

C_UP = 128
C_HID = 64
C_VEL = 3
SIZE_X, SIZE_Y, SIZE_Z = 8, 16, 4
CELLS = SIZE_X * SIZE_Y * SIZE_Z
NORM = 1.0 / 512.0
F32, BF16 = jnp.float32, jnp.bfloat16

GX, GY, GZ = "gx", "gy", ("gzh", "gzm", "gzl")
PLANE = ("gx", "gy")
NEAR = ("gzh", "gzl")
FAR = "gzm"
BLOCKS = 16
OWN = C_HID // BLOCKS
ROWS = 6 * OWN
SHARE = (32, OWN * 192)
HIGHEST = lax.Precision.HIGHEST


root_half = 0.7071067811865476
inv_root_tau = 0.3989422804014327


def gelu_value(values):
    return 0.5 * values * (1.0 + lax.erf(values * root_half))


def gelu_slope(values):
    return (
        0.5 * (1.0 + lax.erf(values * root_half))
        + values * jnp.exp(-0.5 * values * values) * inv_root_tau
    )


def from_both(to_next, to_previous, axis):
    peers = lax.axis_size(axis)
    up = [(i, (i + 1) % peers) for i in range(peers)]
    down = [(j, i) for i, j in up]
    return lax.ppermute(to_next, axis, up), lax.ppermute(to_previous, axis, down)


def depth_rims(pre_act, cotangent):
    cot = jnp.transpose(cotangent, (3, 0, 1, 2)).reshape(SIZE_Z * C_VEL, 128)
    cot = jnp.pad(cot, ((0, 4), (0, 0)))
    rows, high, low = pl.pallas_call(
        turn_kernel,
        out_shape=(
            jax.ShapeDtypeStruct((272, 128), BF16),
            jax.ShapeDtypeStruct((80, 128), BF16),
            jax.ShapeDtypeStruct((80, 128), BF16),
        ),
        compiler_params=pltpu.CompilerParams(vmem_limit_bytes=8 * 2**20),
    )(pre_act.reshape(128, SIZE_Z * C_HID), cot)
    before, after = from_both(high, low, GZ)
    return before, rows, after


def plane_inputs(coarse, skip_features):
    parts = pl.pallas_call(
        message_kernel,
        out_shape=jax.ShapeDtypeStruct((BLOCKS, 160, 256), BF16),
        out_specs=pl.BlockSpec(memory_space=pl.ANY),
        scratch_shapes=[pltpu.SemaphoreType.DMA((2, BLOCKS))],
        compiler_params=pltpu.CompilerParams(vmem_limit_bytes=8 * 2**20),
    )(coarse.reshape(32, 256), skip_features.reshape(128, 256))
    return traded(parts, PLANE)


def with_x_rims(field):
    before, after = from_both(field[6:], field[:2], GX)
    return jnp.concatenate([before, field, after], axis=0)


def with_y_rims(field):
    before, after = from_both(field[:, 14:], field[:, :2], GY)
    fill = jnp.zeros((SIZE_X + 4, 12, 512), BF16)
    return jnp.concatenate([before, field, after, fill], axis=1)


def head_matrix(weight_out):
    taps = weight_out.reshape(9, 3, C_VEL, C_HID)[:, ::-1].reshape(9, 9, C_HID)
    columns = [jnp.pad(taps, ((0, 0), (3 * z, 23 - 3 * z), (0, 0))) for z in range(6)]
    return jnp.concatenate(columns, axis=2)


def own_head_matrix(head):
    place = lax.axis_index(GX) * lax.axis_size(GY) + lax.axis_index(GY)
    split = head[:, :24].reshape(9, 24, 6, BLOCKS, OWN)
    own = lax.dynamic_index_in_dim(split, place, 3, keepdims=False)
    return jnp.transpose(own, (2, 3, 0, 1)).reshape(ROWS, 216)


def row_choices():
    shares = np.zeros((BLOCKS, 6, OWN, 384), np.float32)
    cots = np.zeros((128, 48), np.float32)
    for z in range(6):
        for c in range(C_HID):
            shares[c // OWN, z, c % OWN, C_HID * z + c] = 1.0
    for z in range(-2, 6):
        start = 12 + 3 * z if z < 0 else 20 + 3 * z if z > 3 else 16 + 3 * z
        for o in range(C_VEL):
            cots[C_VEL * (z + 2) + o, start + o] = 1.0
    return jnp.asarray(shares.reshape(384, 384), BF16), jnp.asarray(cots, BF16)


def choices():
    tap_rows = np.zeros((2, 2, OWN, 32, 216), np.float32)
    head_columns = np.zeros((9, 8, C_VEL, SIZE_Z, 128), np.float32)
    for tap in range(27):
        pair, c = tap // 3, tap % 3 - 1
        for z in range(SIZE_Z):
            for own in range(OWN):
                row = ROWS * pair + OWN * (z + 1 - c) + own
                tap_rows[z // 2, z % 2, own, tap, row] = 1.0
            for o in range(C_VEL):
                head_columns[pair, z + 2 - c, o, z, 32 * o + tap] = 1.0
    head_rows = np.zeros((32, 6, OWN), np.float32)
    for own in range(OWN):
        head_rows[27 + own, 1:5, own] = 1.0
    double = np.zeros((SIZE_X, SIZE_Y, SIZE_X // 2, SIZE_Y // 2), np.float32)
    for x in range(SIZE_X):
        for y in range(SIZE_Y):
            double[x, y, x // 2, y // 2] = 1.0
    return (
        jnp.asarray(tap_rows.reshape(2, 256, 216), BF16),
        jnp.asarray(head_columns.reshape(216, 512), BF16),
        jnp.asarray(head_rows.reshape(32, ROWS)),
    ), jnp.asarray(double.reshape(128, 32), BF16)


def head_channels():
    rows = np.zeros((BLOCKS, 32, C_HID), np.float32)
    for at in range(BLOCKS):
        for own in range(OWN):
            rows[at, 27 + own, OWN * at + own] = 1.0
    return jnp.asarray(rows.reshape(512, C_HID), BF16)


def turn_kernel(pre_ref, cot_ref, rows_ref, high_ref, low_ref):
    turned = pre_ref[...].astype(F32).T.astype(BF16)
    rows_ref[0:256, :] = turned
    rows_ref[256:272, :] = cot_ref[...]
    high_ref[0:64, :] = turned[192:256]
    high_ref[64:80, :] = cot_ref[...]
    low_ref[0:64, :] = turned[0:64]
    low_ref[64:80, :] = cot_ref[...]


def joined(before_ref, rows_ref, after_ref, cot_choice_ref):
    pre = jnp.concatenate([before_ref[0:64, :], rows_ref[0:256, :], after_ref[0:64, :]], axis=0)
    cot = jnp.concatenate(
        [before_ref[64:80, :], rows_ref[256:272, :], after_ref[64:80, :]], axis=0
    )
    return pre, jnp.dot(cot_choice_ref[...], cot, preferred_element_type=F32)


def parts_kernel(before_ref, rows_ref, after_ref, choice_ref, cot_choice_ref, parts_ref):
    pre, cot = joined(before_ref, rows_ref, after_ref, cot_choice_ref)
    parts = jnp.dot(choice_ref[...], pre, preferred_element_type=F32)
    for at in range(BLOCKS):
        both = jnp.concatenate([parts[ROWS * at : ROWS * at + ROWS], cot[0:24]], axis=0)
        parts_ref[at] = both.astype(BF16)


def field_kernel(before_ref, rows_ref, after_ref, cot_choice_ref, field_ref):
    pre, cot = joined(before_ref, rows_ref, after_ref, cot_choice_ref)
    field = jnp.concatenate([pre.astype(F32), cot], axis=0).T
    field_ref[...] = field.astype(BF16).reshape(SIZE_X, SIZE_Y, 512)


def unpack_kernel(share_ref, choice_ref, body_ref, head_ref):
    for at in range(BLOCKS):
        wide = share_ref[at].astype(F32) * NORM
        body_ref[:, 768 * at : 768 * at + 768] = wide[0:27]
    rows = share_ref[:, :, 0:128].reshape(512, 128)
    head = lax.dot_general(
        rows, choice_ref[...], (((0,), (0,)), ((), ())), preferred_element_type=F32
    )
    for o in range(C_VEL):
        head_ref[o] = head[32 * o : 32 * o + 27] * NORM


def input_matrix(weight_one):
    taps = weight_one.reshape(9, 3, C_HID, 192)[:, ::-1].reshape(9, 192, 192)
    wide = jnp.concatenate([taps, taps[..., C_UP:]], axis=2)
    return jnp.pad(wide, ((0, 0), (0, 64), (0, 0)))


def low_half(shape):
    return lax.broadcasted_iota(jnp.int32, shape, len(shape) - 1) < 64


def rolled(values, shift):
    flat = values.reshape(-1, values.shape[-1])
    return pltpu.roll(flat, shift, 1).reshape(values.shape)


def moved_y(blocks, b, lane):
    if b == 0:
        return blocks
    out = []
    for at in range(BLOCKS):
        gx, gy = at // 4, at % 4
        there = blocks[4 * gx + (gy - b) % 4]
        edge = lane % 16 == (0 if b == 1 else 15)
        out.append(
            jnp.where(edge, pltpu.roll(there, -15 * b % 128, 1), pltpu.roll(blocks[at], b % 128, 1))
        )
    return out


def moved_x(blocks, a, lane):
    if a == 0:
        return blocks
    turned = [pltpu.roll(block, 16 * a % 128, 1) for block in blocks]
    edge = lane // 16 == (0 if a == 1 else 7)
    return [
        jnp.where(edge, turned[4 * ((at // 4 - a) % 4) + at % 4], turned[at])
        for at in range(BLOCKS)
    ]


def stack_moved(blocks, stack_ref):
    lane = lax.broadcasted_iota(jnp.int32, (ROWS, 128), 1)
    for b in (-1, 0, 1):
        rows = moved_y(blocks, b, lane)
        for a in (-1, 0, 1):
            start = ROWS * (3 * (a + 1) + b + 1)
            for at, block in enumerate(moved_x(rows, a, lane)):
                stack_ref[start : start + ROWS, 128 * at : 128 * at + 128] = block


def message_kernel(coarse_ref, skip_ref, parts_ref, sems):
    copies = []
    for at in range(BLOCKS):
        copies.append(
            pltpu.make_async_copy(coarse_ref, parts_ref.at[at, 0:32, :], sems.at[0, at])
        )
        copies.append(
            pltpu.make_async_copy(skip_ref, parts_ref.at[at, 32:160, :], sems.at[1, at])
        )
    for copy in copies:
        copy.start()
    for copy in copies:
        copy.wait()


def fine_kernel(input_ref, double_ref, fine_ref):
    for at in range(BLOCKS):
        rows = slice(128 * at, 128 * at + 128)
        fine = jnp.dot(double_ref[...], input_ref[at, 0:32, :], preferred_element_type=F32)
        for pair in range(2):
            lanes = slice(128 * pair, 128 * pair + 128)
            fine_ref[pair, rows, 0:128] = fine[:, lanes].astype(BF16)
            fine_ref[pair, rows, 128:256] = input_ref[at, 32:160, lanes]


def share_kernel(data_ref, fine_ref, head_ref, tap_ref, column_ref, row_ref, share_ref, stack_s):
    blocks = [data_ref[at].astype(F32) for at in range(BLOCKS)]
    stack_moved([block[ROWS:48] for block in blocks], stack_s)
    cot = stack_s[...].astype(BF16)
    pre = jnp.concatenate([block[0:ROWS] for block in blocks], axis=1)
    d_hidden = jnp.dot(head_ref[...], cot, preferred_element_type=F32)
    d_pre = (d_hidden * gelu_slope(pre)).astype(BF16).astype(F32)
    hidden = gelu_value(pre).astype(BF16)
    pairs = lax.dot_general(hidden, cot, (((1,), (1,)), ((), ())), preferred_element_type=F32)
    spans = jnp.dot(
        pairs, column_ref[...].astype(F32), precision=HIGHEST, preferred_element_type=F32
    )
    depth = lax.broadcasted_iota(jnp.int32, (ROWS, 128), 0) // OWN
    kept = jnp.zeros((ROWS, 128), F32)
    for z in range(SIZE_Z):
        kept = jnp.where(depth == z + 1, spans[:, 128 * z : 128 * z + 128], kept)
    head = jnp.dot(row_ref[...], kept, precision=HIGHEST, preferred_element_type=F32)

    stack_moved([d_pre[:, 128 * at : 128 * at + 128] for at in range(BLOCKS)], stack_s)
    back = stack_s[...].astype(BF16)
    up = jnp.zeros((128, 128), F32)
    skip = jnp.zeros((128, 128), F32)
    for pair in range(2):
        result = jnp.dot(back, fine_ref[pair], preferred_element_type=F32)
        taps = jnp.dot(
            tap_ref[pair].astype(F32), result, precision=HIGHEST, preferred_element_type=F32
        )
        up = up + taps[0:128, 0:128] + taps[128:256, 0:128]
        skip = skip + taps[0:128, 128:256] + rolled(taps[128:256, 128:256], 64)
    half = low_half((32, 128))
    for even in range(0, OWN, 2):
        first, second = slice(32 * even, 32 * even + 32), slice(32 * even + 32, 32 * even + 64)
        turned = rolled(up[second], 64)
        start = 192 * even
        share_ref[:, start : start + 128] = up[first] + head if even == 0 else up[first]
        share_ref[:, start + 128 : start + 256] = jnp.where(half, skip[first], turned)
        share_ref[:, start + 256 : start + 384] = jnp.where(half, turned, rolled(skip[second], 64))


def input_kernel(field_ref, head_ref, weight_ref, skip_ref, coarse_ref, cot_s, pre_s, window_s, sum_s):
    cot_s[:, 0:8, :] = jnp.zeros((12, 8, 128), F32)
    cot_s[:, 8:40, :] = field_ref[:, :, 384:512].astype(F32)
    total = jnp.zeros((240, 384), F32)
    for a in (-1, 0, 1):
        for b in (-1, 0, 1):
            moved = cot_s[1 - a : 11 - a, 8 - b : 32 - b, :].reshape(240, 128).astype(BF16)
            total = total + jnp.dot(
                moved[:, :32], head_ref[3 * (a + 1) + b + 1], preferred_element_type=F32
            )
    pre_wide = field_ref[1:11, :, 0:384].astype(F32)[:, :24].reshape(240, 384)
    d_pre = (total * gelu_slope(pre_wide)).astype(BF16).astype(F32)
    pre_s[...] = d_pre.reshape(10, 24, 384)

    half = low_half((10, 16, 128))
    for b in (-1, 0, 1):
        moved = pre_s[:, 2 - b : 18 - b, :]
        shifted = rolled(moved, 320)
        for z in range(SIZE_Z):
            source, start = (moved, 64 * z) if z % 2 == 0 else (shifted, 64 * z - 64)
            low = source[:, :, start : start + 128]
            high = jnp.where(half, source[:, :, start + 128 : start + 256], 0.0)
            window_s[b + 1, z, :, :, 0:128] = low.astype(BF16)
            window_s[b + 1, z, :, :, 128:256] = high.astype(BF16)

    windows = [
        window_s[b + 1, :, 1 - a : 9 - a].reshape(CELLS, 256)
        for a in (-1, 0, 1)
        for b in (-1, 0, 1)
    ]
    total = jnp.dot(
        jnp.concatenate(windows, axis=1),
        weight_ref[...].reshape(9 * 256, 256),
        preferred_element_type=F32,
    ).reshape(SIZE_Z, SIZE_X, SIZE_Y, 256)
    half = low_half((8, 16, 128))
    for pair in range(2):
        even, odd = total[2 * pair], total[2 * pair + 1]
        lanes = slice(128 * pair, 128 * pair + 128)
        skip_ref[:, :, lanes] = jnp.where(half, even[..., 128:], odd[..., 128:]).astype(BF16)
        both = (even[..., :128] + odd[..., :128]).reshape(4, 2, 16, 128)
        sum_s[...] = (both[:, 0] + both[:, 1]).reshape(64, 128)
        summed = sum_s[pl.ds(0, 32, stride=2), :] + sum_s[pl.ds(1, 32, stride=2), :]
        coarse_ref[:, lanes] = summed.astype(BF16)


def traded(parts, axes):
    return lax.all_to_all(parts, axes, 0, 0)


def spread(part, axes):
    peers = lax.axis_size(axes)
    return traded(jnp.broadcast_to(part[None], (peers, *part.shape)), axes)


def per_device(coarse, skip_features, pre_act, cotangent, weight_one, weight_out):
    inputs = plane_inputs(coarse, skip_features)
    head = head_matrix(weight_out)
    deep = depth_rims(pre_act, cotangent)
    share_choice, cot_choice = row_choices()
    parts = pl.pallas_call(
        parts_kernel,
        out_shape=jax.ShapeDtypeStruct((BLOCKS, 48, 128), BF16),
        compiler_params=pltpu.CompilerParams(vmem_limit_bytes=8 * 2**20),
    )(*deep, share_choice, cot_choice)
    parts, inputs = lax.optimization_barrier((parts, inputs))
    data = traded(parts, PLANE)
    chosen, double = choices()
    fine = pl.pallas_call(
        fine_kernel,
        out_shape=jax.ShapeDtypeStruct((2, 2048, 256), BF16),
        compiler_params=pltpu.CompilerParams(vmem_limit_bytes=16 * 2**20),
        cost_estimate=pl.CostEstimate(
            flops=300_000_000, bytes_accessed=4_000_000, transcendentals=0
        ),
    )(inputs, double)
    field = pl.pallas_call(
        field_kernel,
        out_shape=jax.ShapeDtypeStruct((SIZE_X, SIZE_Y, 512), BF16),
        compiler_params=pltpu.CompilerParams(vmem_limit_bytes=8 * 2**20),
        cost_estimate=pl.CostEstimate(
            flops=60_000_000, bytes_accessed=4_000_000, transcendentals=0
        ),
    )(*deep, cot_choice)
    data, fine, field = lax.optimization_barrier((data, fine, field))
    share = pl.pallas_call(
        share_kernel,
        out_shape=jax.ShapeDtypeStruct(SHARE, F32),
        scratch_shapes=[pltpu.VMEM((216, 2048), F32)],
        compiler_params=pltpu.CompilerParams(vmem_limit_bytes=32 * 2**20),
        cost_estimate=pl.CostEstimate(
            flops=1_500_000_000, bytes_accessed=2_000_000, transcendentals=200_000
        ),
    )(data, fine, own_head_matrix(head), *chosen)
    near = jnp.sum(traded(share.reshape(4, 8, SHARE[1]), NEAR), axis=0)
    field, near = lax.optimization_barrier((field, near))
    field = with_x_rims(field)
    far = jnp.sum(spread(near.astype(BF16), FAR).astype(F32), axis=0)
    field, far = lax.optimization_barrier((field, far))
    field = with_y_rims(field)
    column = spread(far, NEAR).reshape(SHARE)
    field, column = lax.optimization_barrier((field, column))
    body, head_grad = pl.pallas_call(
        unpack_kernel,
        out_shape=(
            jax.ShapeDtypeStruct((27, C_HID * 192), F32),
            jax.ShapeDtypeStruct((C_VEL, 27, C_HID), F32),
        ),
        compiler_params=pltpu.CompilerParams(vmem_limit_bytes=16 * 2**20),
    )(spread(column.astype(BF16), PLANE), head_channels())
    skip_grad, coarse_grad = pl.pallas_call(
        input_kernel,
        out_shape=(
            jax.ShapeDtypeStruct((SIZE_X, SIZE_Y, 256), BF16),
            jax.ShapeDtypeStruct((32, 256), BF16),
        ),
        scratch_shapes=[
            pltpu.VMEM((12, 40, 128), F32),
            pltpu.VMEM((10, 24, 384), F32),
            pltpu.VMEM((3, SIZE_Z, 10, 16, 256), BF16),
            pltpu.VMEM((64, 128), F32),
        ],
        compiler_params=pltpu.CompilerParams(vmem_limit_bytes=32 * 2**20),
        cost_estimate=pl.CostEstimate(
            flops=700_000_000, bytes_accessed=3_000_000, transcendentals=100_000
        ),
    )(field, head, input_matrix(weight_one))
    return coarse_grad.reshape(4, 8, 256), skip_grad, body, jnp.transpose(head_grad, (1, 0, 2))


def solution(mesh):
    names = ("gx", "gy", "gzh", "gzm", "gzl")
    split = Mesh(mesh.devices.reshape(4, 4, 2, 8, 2), names)
    field = P("gx", "gy", GZ)
    return jax.shard_map(
        per_device,
        mesh=split,
        in_specs=(field, field, field, P(None, "gx", "gy", GZ), P(), P()),
        out_specs=(field, field, P(), P()),
        check_vma=False,
    )
```

```python
import jax
import jax.numpy as jnp
import numpy as np
from jax import lax
from jax.experimental import pallas as pl
from jax.experimental.pallas import tpu as pltpu
from jax.sharding import Mesh, PartitionSpec as P

C_UP = 128
C_HID = 64
C_VEL = 3
SIZE_X, SIZE_Y, SIZE_Z = 8, 16, 4
CELLS = SIZE_X * SIZE_Y * SIZE_Z
NORM = 1.0 / 512.0
F32, BF16 = jnp.float32, jnp.bfloat16

GX, GY, GZ = "gx", "gy", ("gzh", "gzm", "gzl")
PLANE = ("gx", "gy")
NEAR = ("gzh", "gzl")
FAR = "gzm"
BLOCKS = 16
OWN = C_HID // BLOCKS
ROWS = 6 * OWN
SHARE = (32, OWN * 192)
HIGHEST = lax.Precision.HIGHEST


root_half = 0.7071067811865476
inv_root_tau = 0.3989422804014327


def gelu_value(values):
    return 0.5 * values * (1.0 + lax.erf(values * root_half))


def gelu_slope(values):
    return (
        0.5 * (1.0 + lax.erf(values * root_half))
        + values * jnp.exp(-0.5 * values * values) * inv_root_tau
    )


def from_both(to_next, to_previous, axis):
    peers = lax.axis_size(axis)
    up = [(i, (i + 1) % peers) for i in range(peers)]
    down = [(j, i) for i, j in up]
    return lax.ppermute(to_next, axis, up), lax.ppermute(to_previous, axis, down)


def depth_rims(pre_act, cotangent):
    cot = jnp.transpose(cotangent, (3, 0, 1, 2)).reshape(SIZE_Z * C_VEL, 128)
    cot = jnp.pad(cot, ((0, 4), (0, 0)))
    rows, high, low = pl.pallas_call(
        turn_kernel,
        out_shape=(
            jax.ShapeDtypeStruct((272, 128), BF16),
            jax.ShapeDtypeStruct((80, 128), BF16),
            jax.ShapeDtypeStruct((80, 128), BF16),
        ),
        compiler_params=pltpu.CompilerParams(vmem_limit_bytes=8 * 2**20),
    )(pre_act.reshape(128, SIZE_Z * C_HID), cot)
    before, after = from_both(high, low, GZ)
    return before, rows, after


def plane_inputs(coarse, skip_features):
    parts = pl.pallas_call(
        message_kernel,
        out_shape=jax.ShapeDtypeStruct((BLOCKS, 160, 256), BF16),
        in_specs=[pl.BlockSpec(memory_space=pltpu.HBM)] * 2,
        out_specs=pl.BlockSpec(memory_space=pltpu.HBM),
        scratch_shapes=[pltpu.SemaphoreType.DMA((2, BLOCKS))],
        compiler_params=pltpu.CompilerParams(vmem_limit_bytes=8 * 2**20),
    )(coarse.reshape(32, 256), skip_features.reshape(128, 256))
    return traded(parts, PLANE)


def with_x_rims(field):
    before, after = from_both(field[6:], field[:2], GX)
    return jnp.concatenate([before, field, after], axis=0)


def with_y_rims(field):
    before, after = from_both(field[:, 14:], field[:, :2], GY)
    fill = jnp.zeros((SIZE_X + 4, 12, 512), BF16)
    return jnp.concatenate([before, field, after, fill], axis=1)


def head_matrix(weight_out):
    taps = weight_out.reshape(9, 3, C_VEL, C_HID)[:, ::-1].reshape(9, 9, C_HID)
    columns = [jnp.pad(taps, ((0, 0), (3 * z, 23 - 3 * z), (0, 0))) for z in range(6)]
    return jnp.concatenate(columns, axis=2)


def own_head_matrix(head):
    place = lax.axis_index(GX) * lax.axis_size(GY) + lax.axis_index(GY)
    split = head[:, :24].reshape(9, 24, 6, BLOCKS, OWN)
    own = lax.dynamic_index_in_dim(split, place, 3, keepdims=False)
    return jnp.transpose(own, (2, 3, 0, 1)).reshape(ROWS, 216)


def row_choices():
    shares = np.zeros((BLOCKS, 6, OWN, 384), np.float32)
    cots = np.zeros((128, 48), np.float32)
    for z in range(6):
        for c in range(C_HID):
            shares[c // OWN, z, c % OWN, C_HID * z + c] = 1.0
    for z in range(-2, 6):
        start = 12 + 3 * z if z < 0 else 20 + 3 * z if z > 3 else 16 + 3 * z
        for o in range(C_VEL):
            cots[C_VEL * (z + 2) + o, start + o] = 1.0
    return jnp.asarray(shares.reshape(384, 384), BF16), jnp.asarray(cots, BF16)


def choices():
    tap_rows = np.zeros((2, 2, OWN, 32, 216), np.float32)
    head_columns = np.zeros((9, 8, C_VEL, SIZE_Z, 128), np.float32)
    for tap in range(27):
        pair, c = tap // 3, tap % 3 - 1
        for z in range(SIZE_Z):
            for own in range(OWN):
                row = ROWS * pair + OWN * (z + 1 - c) + own
                tap_rows[z // 2, z % 2, own, tap, row] = 1.0
            for o in range(C_VEL):
                head_columns[pair, z + 2 - c, o, z, 32 * o + tap] = 1.0
    double = np.zeros((SIZE_X, SIZE_Y, SIZE_X // 2, SIZE_Y // 2), np.float32)
    for x in range(SIZE_X):
        for y in range(SIZE_Y):
            double[x, y, x // 2, y // 2] = 1.0
    return (
        jnp.asarray(tap_rows.reshape(2, 256, 216), BF16),
        jnp.asarray(head_columns.reshape(216, 512), BF16),
    ), jnp.asarray(double.reshape(128, 32), BF16)


def head_channels():
    rows = np.zeros((BLOCKS, 32, C_HID), np.float32)
    for at in range(BLOCKS):
        for own in range(OWN):
            rows[at, 27 + own, OWN * at + own] = 1.0
    return jnp.asarray(rows.reshape(512, C_HID), BF16)


def turn_kernel(pre_ref, cot_ref, rows_ref, high_ref, low_ref):
    turned = pre_ref[...].astype(F32).T.astype(BF16)
    rows_ref[0:256, :] = turned
    rows_ref[256:272, :] = cot_ref[...]
    high_ref[0:64, :] = turned[192:256]
    high_ref[64:80, :] = cot_ref[...]
    low_ref[0:64, :] = turned[0:64]
    low_ref[64:80, :] = cot_ref[...]


def joined(before_ref, rows_ref, after_ref, cot_choice_ref):
    pre = jnp.concatenate([before_ref[0:64, :], rows_ref[0:256, :], after_ref[0:64, :]], axis=0)
    cot = jnp.concatenate(
        [before_ref[64:80, :], rows_ref[256:272, :], after_ref[64:80, :]], axis=0
    )
    return pre, jnp.dot(cot_choice_ref[...], cot, preferred_element_type=F32)


def parts_kernel(before_ref, rows_ref, after_ref, choice_ref, cot_choice_ref, parts_ref):
    pre, cot = joined(before_ref, rows_ref, after_ref, cot_choice_ref)
    parts = jnp.dot(choice_ref[...], pre, preferred_element_type=F32)
    for at in range(BLOCKS):
        both = jnp.concatenate([parts[ROWS * at : ROWS * at + ROWS], cot[0:24]], axis=0)
        parts_ref[at] = both.astype(BF16)


def field_kernel(before_ref, rows_ref, after_ref, cot_choice_ref, field_ref):
    pre, cot = joined(before_ref, rows_ref, after_ref, cot_choice_ref)
    field = jnp.concatenate([pre.astype(F32), cot], axis=0).T
    field_ref[...] = field.astype(BF16).reshape(SIZE_X, SIZE_Y, 512)


def unpack_kernel(share_ref, choice_ref, body_ref, head_ref):
    for at in range(BLOCKS):
        wide = share_ref[at].astype(F32) * NORM
        body_ref[:, 768 * at : 768 * at + 768] = wide[0:27]
    rows = share_ref[:, :, 0:128].reshape(512, 128)
    head = lax.dot_general(
        rows, choice_ref[...], (((0,), (0,)), ((), ())), preferred_element_type=F32
    )
    for o in range(C_VEL):
        head_ref[o] = head[32 * o : 32 * o + 27] * NORM


def input_matrix(weight_one):
    taps = weight_one.reshape(9, 3, C_HID, 192)[:, ::-1].reshape(9, 192, 192)
    wide = jnp.concatenate([taps, taps[..., C_UP:]], axis=2)
    return jnp.pad(wide, ((0, 0), (0, 64), (0, 0)))


def low_half(shape):
    return lax.broadcasted_iota(jnp.int32, shape, len(shape) - 1) < 64


def rolled(values, shift):
    flat = values.reshape(-1, values.shape[-1])
    return pltpu.roll(flat, shift, 1).reshape(values.shape)


def moved_y(blocks, b, lane):
    if b == 0:
        return blocks
    out = []
    for at in range(BLOCKS):
        gx, gy = at // 4, at % 4
        there = blocks[4 * gx + (gy - b) % 4]
        edge = lane % 16 == (0 if b == 1 else 15)
        out.append(
            jnp.where(edge, pltpu.roll(there, -15 * b % 128, 1), pltpu.roll(blocks[at], b % 128, 1))
        )
    return out


def moved_x(blocks, a, lane):
    if a == 0:
        return blocks
    turned = [pltpu.roll(block, 16 * a % 128, 1) for block in blocks]
    edge = lane // 16 == (0 if a == 1 else 7)
    return [
        jnp.where(edge, turned[4 * ((at // 4 - a) % 4) + at % 4], turned[at])
        for at in range(BLOCKS)
    ]


def stack_moved(blocks, stack_ref):
    lane = lax.broadcasted_iota(jnp.int32, (ROWS, 128), 1)
    for b in (-1, 0, 1):
        rows = moved_y(blocks, b, lane)
        for a in (-1, 0, 1):
            start = ROWS * (3 * (a + 1) + b + 1)
            for at, block in enumerate(moved_x(rows, a, lane)):
                stack_ref[start : start + ROWS, 128 * at : 128 * at + 128] = block


def message_kernel(coarse_ref, skip_ref, parts_ref, sems):
    copies = []
    for at in range(BLOCKS):
        copies.append(
            pltpu.make_async_copy(coarse_ref, parts_ref.at[at, 0:32, :], sems.at[0, at])
        )
        copies.append(
            pltpu.make_async_copy(skip_ref, parts_ref.at[at, 32:160, :], sems.at[1, at])
        )
    for copy in copies:
        copy.start()
    for copy in copies:
        copy.wait()


def fine_kernel(input_ref, double_ref, fine_ref):
    for at in range(BLOCKS):
        rows = slice(128 * at, 128 * at + 128)
        fine = jnp.dot(double_ref[...], input_ref[at, 0:32, :], preferred_element_type=F32)
        for pair in range(2):
            lanes = slice(128 * pair, 128 * pair + 128)
            fine_ref[pair, rows, 0:128] = fine[:, lanes].astype(BF16)
            fine_ref[pair, rows, 128:256] = input_ref[at, 32:160, lanes]


def share_kernel(
    data_ref, fine_hbm, head_ref, tap_hbm, column_hbm, share_ref, stack_s, fine_ref, tap_ref, column_ref, sems
):
    column_copy = pltpu.make_async_copy(column_hbm, column_ref, sems.at[0])
    tap_copy = pltpu.make_async_copy(tap_hbm, tap_ref, sems.at[1])
    fine_copy = pltpu.make_async_copy(fine_hbm, fine_ref, sems.at[2])
    column_copy.start()
    fine_copy.start()
    tap_copy.start()
    blocks = [data_ref[at].astype(F32) for at in range(BLOCKS)]
    stack_moved([block[ROWS:48] for block in blocks], stack_s)
    cot = stack_s[...].astype(BF16)
    pre = jnp.concatenate([block[0:ROWS] for block in blocks], axis=1)
    d_hidden = jnp.dot(head_ref[...], cot, preferred_element_type=F32)
    d_pre = (d_hidden * gelu_slope(pre)).astype(BF16).astype(F32)
    hidden = gelu_value(pre).astype(BF16)
    pairs = lax.dot_general(hidden, cot, (((1,), (1,)), ((), ())), preferred_element_type=F32)
    column_copy.wait()
    spans = jnp.dot(
        pairs, column_ref[...].astype(F32), precision=HIGHEST, preferred_element_type=F32
    )
    depth = lax.broadcasted_iota(jnp.int32, (ROWS, 128), 0) // OWN
    kept = jnp.zeros((ROWS, 128), F32)
    for z in range(SIZE_Z):
        kept = jnp.where(depth == z + 1, spans[:, 128 * z : 128 * z + 128], kept)
    row = lax.broadcasted_iota(jnp.int32, (32, ROWS), 0) - 27
    source = lax.broadcasted_iota(jnp.int32, (32, ROWS), 1)
    place = jnp.where(source % OWN == row, 1.0, 0.0).astype(F32)
    head = jnp.dot(place, kept, precision=HIGHEST, preferred_element_type=F32)

    stack_moved([d_pre[:, 128 * at : 128 * at + 128] for at in range(BLOCKS)], stack_s)
    back = stack_s[...].astype(BF16)
    fine_copy.wait()
    tap_copy.wait()
    up = jnp.zeros((128, 128), F32)
    skip = jnp.zeros((128, 128), F32)
    for pair in range(2):
        result = jnp.dot(back, fine_ref[pair], preferred_element_type=F32)
        taps = jnp.dot(
            tap_ref[pair].astype(F32), result, precision=HIGHEST, preferred_element_type=F32
        )
        up = up + taps[0:128, 0:128] + taps[128:256, 0:128]
        skip = skip + taps[0:128, 128:256] + rolled(taps[128:256, 128:256], 64)
    half = low_half((32, 128))
    for even in range(0, OWN, 2):
        first, second = slice(32 * even, 32 * even + 32), slice(32 * even + 32, 32 * even + 64)
        turned = rolled(up[second], 64)
        start = 192 * even
        share_ref[:, start : start + 128] = up[first] + head if even == 0 else up[first]
        share_ref[:, start + 128 : start + 256] = jnp.where(half, skip[first], turned)
        share_ref[:, start + 256 : start + 384] = jnp.where(half, turned, rolled(skip[second], 64))


def input_kernel(field_ref, head_ref, weight_ref, skip_ref, coarse_ref, cot_s, pre_s, window_s, sum_s):
    cot_s[:, 0:8, :] = jnp.zeros((12, 8, 128), F32)
    cot_s[:, 8:40, :] = field_ref[:, :, 384:512].astype(F32)
    total = jnp.zeros((240, 384), F32)
    for a in (-1, 0, 1):
        for b in (-1, 0, 1):
            moved = cot_s[1 - a : 11 - a, 8 - b : 32 - b, :].reshape(240, 128).astype(BF16)
            total = total + jnp.dot(
                moved[:, :32], head_ref[3 * (a + 1) + b + 1], preferred_element_type=F32
            )
    pre_wide = field_ref[1:11, :, 0:384].astype(F32)[:, :24].reshape(240, 384)
    d_pre = (total * gelu_slope(pre_wide)).astype(BF16).astype(F32)
    pre_s[...] = d_pre.reshape(10, 24, 384)

    half = low_half((10, 16, 128))
    for b in (-1, 0, 1):
        moved = pre_s[:, 2 - b : 18 - b, :]
        shifted = rolled(moved, 320)
        for z in range(SIZE_Z):
            source, start = (moved, 64 * z) if z % 2 == 0 else (shifted, 64 * z - 64)
            low = source[:, :, start : start + 128]
            high = jnp.where(half, source[:, :, start + 128 : start + 256], 0.0)
            window_s[b + 1, z, :, :, 0:128] = low.astype(BF16)
            window_s[b + 1, z, :, :, 128:256] = high.astype(BF16)

    windows = [
        window_s[b + 1, :, 1 - a : 9 - a].reshape(CELLS, 256)
        for a in (-1, 0, 1)
        for b in (-1, 0, 1)
    ]
    total = jnp.dot(
        jnp.concatenate(windows, axis=1),
        weight_ref[...].reshape(9 * 256, 256),
        preferred_element_type=F32,
    ).reshape(SIZE_Z, SIZE_X, SIZE_Y, 256)
    half = low_half((8, 16, 128))
    for pair in range(2):
        even, odd = total[2 * pair], total[2 * pair + 1]
        lanes = slice(128 * pair, 128 * pair + 128)
        skip_ref[:, :, lanes] = jnp.where(half, even[..., 128:], odd[..., 128:]).astype(BF16)
        both = (even[..., :128] + odd[..., :128]).reshape(4, 2, 16, 128)
        sum_s[...] = (both[:, 0] + both[:, 1]).reshape(64, 128)
        summed = sum_s[pl.ds(0, 32, stride=2), :] + sum_s[pl.ds(1, 32, stride=2), :]
        coarse_ref[:, lanes] = summed.astype(BF16)


def traded(parts, axes):
    return lax.all_to_all(parts, axes, 0, 0)


def spread(part, axes):
    peers = lax.axis_size(axes)
    return traded(jnp.broadcast_to(part[None], (peers, *part.shape)), axes)


def per_device(coarse, skip_features, pre_act, cotangent, weight_one, weight_out):
    inputs = plane_inputs(coarse, skip_features)
    head = head_matrix(weight_out)
    deep = depth_rims(pre_act, cotangent)
    share_choice, cot_choice = row_choices()
    parts = pl.pallas_call(
        parts_kernel,
        out_shape=jax.ShapeDtypeStruct((BLOCKS, 48, 128), BF16),
        compiler_params=pltpu.CompilerParams(vmem_limit_bytes=8 * 2**20),
    )(*deep, share_choice, cot_choice)
    parts, inputs = lax.optimization_barrier((parts, inputs))
    data = traded(parts, PLANE)
    chosen, double = choices()
    fine = pl.pallas_call(
        fine_kernel,
        out_shape=jax.ShapeDtypeStruct((2, 2048, 256), BF16),
        compiler_params=pltpu.CompilerParams(vmem_limit_bytes=16 * 2**20),
        cost_estimate=pl.CostEstimate(
            flops=300_000_000, bytes_accessed=4_000_000, transcendentals=0
        ),
    )(inputs, double)
    field = pl.pallas_call(
        field_kernel,
        out_shape=jax.ShapeDtypeStruct((SIZE_X, SIZE_Y, 512), BF16),
        compiler_params=pltpu.CompilerParams(vmem_limit_bytes=8 * 2**20),
        cost_estimate=pl.CostEstimate(
            flops=60_000_000, bytes_accessed=4_000_000, transcendentals=0
        ),
    )(*deep, cot_choice)
    data, fine, field = lax.optimization_barrier((data, fine, field))
    share = pl.pallas_call(
        share_kernel,
        out_shape=jax.ShapeDtypeStruct(SHARE, F32),
        in_specs=[
            pl.BlockSpec(memory_space=pltpu.VMEM),
            pl.BlockSpec(memory_space=pltpu.HBM),
            pl.BlockSpec(memory_space=pltpu.VMEM),
            pl.BlockSpec(memory_space=pltpu.HBM),
            pl.BlockSpec(memory_space=pltpu.HBM),
        ],
        scratch_shapes=[
            pltpu.VMEM((216, 2048), F32),
            pltpu.VMEM((2, 2048, 256), BF16),
            pltpu.VMEM((2, 256, 216), BF16),
            pltpu.VMEM((216, 512), BF16),
            pltpu.SemaphoreType.DMA((3,)),
        ],
        compiler_params=pltpu.CompilerParams(vmem_limit_bytes=32 * 2**20),
        cost_estimate=pl.CostEstimate(
            flops=1_500_000_000, bytes_accessed=2_000_000, transcendentals=200_000
        ),
    )(data, fine, own_head_matrix(head), *chosen)
    near = jnp.sum(traded(share.reshape(4, 8, SHARE[1]), NEAR), axis=0)
    field, near = lax.optimization_barrier((field, near))
    field = with_x_rims(field)
    far = jnp.sum(spread(near.astype(BF16), FAR).astype(F32), axis=0)
    column = spread(far.astype(BF16), NEAR).reshape(SHARE)
    weights = input_matrix(weight_one)
    field, column, weights = lax.optimization_barrier((field, column, weights))
    field = with_y_rims(field)
    body, head_grad = pl.pallas_call(
        unpack_kernel,
        out_shape=(
            jax.ShapeDtypeStruct((27, C_HID * 192), F32),
            jax.ShapeDtypeStruct((C_VEL, 27, C_HID), F32),
        ),
        compiler_params=pltpu.CompilerParams(vmem_limit_bytes=16 * 2**20),
    )(spread(column, PLANE), head_channels())
    skip_grad, coarse_grad = pl.pallas_call(
        input_kernel,
        out_shape=(
            jax.ShapeDtypeStruct((SIZE_X, SIZE_Y, 256), BF16),
            jax.ShapeDtypeStruct((32, 256), BF16),
        ),
        scratch_shapes=[
            pltpu.VMEM((12, 40, 128), F32),
            pltpu.VMEM((10, 24, 384), F32),
            pltpu.VMEM((3, SIZE_Z, 10, 16, 256), BF16),
            pltpu.VMEM((64, 128), F32),
        ],
        compiler_params=pltpu.CompilerParams(vmem_limit_bytes=32 * 2**20),
        cost_estimate=pl.CostEstimate(
            flops=700_000_000, bytes_accessed=3_000_000, transcendentals=100_000
        ),
    )(field, head, weights)
    return coarse_grad.reshape(4, 8, 256), skip_grad, body, jnp.transpose(head_grad, (1, 0, 2))


def solution(mesh):
    names = ("gx", "gy", "gzh", "gzm", "gzl")
    split = Mesh(mesh.devices.reshape(4, 4, 2, 8, 2), names)
    field = P("gx", "gy", GZ)
    return jax.shard_map(
        per_device,
        mesh=split,
        in_specs=(field, field, field, P(None, "gx", "gy", GZ), P(), P()),
        out_specs=(field, field, P(), P()),
        check_vma=False,
    )
```

```python
import jax
import jax.numpy as jnp
import numpy as np
from jax import lax
from jax.experimental import pallas as pl
from jax.experimental.pallas import tpu as pltpu
from jax.sharding import Mesh, PartitionSpec as P

C_UP = 128
C_HID = 64
C_VEL = 3
SIZE_X, SIZE_Y, SIZE_Z = 8, 16, 4
CELLS = SIZE_X * SIZE_Y * SIZE_Z
NORM = 1.0 / 512.0
F32, BF16 = jnp.float32, jnp.bfloat16

GX, GY, GZ = "gx", "gy", ("gzh", "gzm", "gzl")
PLANE = ("gx", "gy")
NEAR = ("gzh", "gzl")
FAR = "gzm"
BLOCKS = 16
OWN = C_HID // BLOCKS
ROWS = 6 * OWN
SHARE = (32, OWN * 192)
HIGHEST = lax.Precision.HIGHEST


root_half = 0.7071067811865476
inv_root_tau = 0.3989422804014327


def gelu_value(values):
    return 0.5 * values * (1.0 + lax.erf(values * root_half))


def gelu_slope(values):
    return (
        0.5 * (1.0 + lax.erf(values * root_half))
        + values * jnp.exp(-0.5 * values * values) * inv_root_tau
    )


def from_both(to_next, to_previous, axis):
    peers = lax.axis_size(axis)
    up = [(i, (i + 1) % peers) for i in range(peers)]
    down = [(j, i) for i, j in up]
    return lax.ppermute(to_next, axis, up), lax.ppermute(to_previous, axis, down)


def depth_rims(pre_act, cotangent):
    cot = jnp.transpose(cotangent, (3, 0, 1, 2)).reshape(SIZE_Z * C_VEL, 128)
    cot = jnp.pad(cot, ((0, 4), (0, 0)))
    rows, high, low = pl.pallas_call(
        turn_kernel,
        out_shape=(
            jax.ShapeDtypeStruct((272, 128), BF16),
            jax.ShapeDtypeStruct((80, 128), BF16),
            jax.ShapeDtypeStruct((80, 128), BF16),
        ),
    )(pre_act.reshape(128, SIZE_Z * C_HID), cot)
    before, after = from_both(high, low, GZ)
    return before, rows, after


def plane_inputs(coarse, skip_features):
    parts = pl.pallas_call(
        message_kernel,
        out_shape=jax.ShapeDtypeStruct((BLOCKS, 160, 256), BF16),
    )(coarse.reshape(32, 256), skip_features.reshape(128, 256))
    return traded(parts, PLANE)


def with_x_rims(field):
    before, after = from_both(field[6:], field[:2], GX)
    return jnp.concatenate([before, field, after], axis=0)


def with_y_rims(field):
    before, after = from_both(field[:, 14:], field[:, :2], GY)
    fill = jnp.zeros((SIZE_X + 4, 12, 512), BF16)
    return jnp.concatenate([before, field, after, fill], axis=1)


def head_matrix(weight_out):
    taps = weight_out.reshape(9, 3, C_VEL, C_HID)[:, ::-1].reshape(9, 9, C_HID)
    columns = [jnp.pad(taps, ((0, 0), (3 * z, 23 - 3 * z), (0, 0))) for z in range(6)]
    return jnp.concatenate(columns, axis=2)


def own_head_matrix(head):
    place = lax.axis_index(GX) * lax.axis_size(GY) + lax.axis_index(GY)
    split = head[:, :24].reshape(9, 24, 6, BLOCKS, OWN)
    own = lax.dynamic_index_in_dim(split, place, 3, keepdims=False)
    return jnp.transpose(own, (2, 3, 0, 1)).reshape(ROWS, 216)


def row_choices():
    shares = np.zeros((BLOCKS, 6, OWN, 384), np.float32)
    cots = np.zeros((128, 48), np.float32)
    for z in range(6):
        for c in range(C_HID):
            shares[c // OWN, z, c % OWN, C_HID * z + c] = 1.0
    for z in range(-2, 6):
        start = 12 + 3 * z if z < 0 else 20 + 3 * z if z > 3 else 16 + 3 * z
        for o in range(C_VEL):
            cots[C_VEL * (z + 2) + o, start + o] = 1.0
    return jnp.asarray(shares.reshape(384, 384), BF16), jnp.asarray(cots, BF16)


def choices():
    tap_rows = np.zeros((2, 2, OWN, 32, 216), np.float32)
    head_columns = np.zeros((9, 8, C_VEL, SIZE_Z, 128), np.float32)
    for tap in range(27):
        pair, c = tap // 3, tap % 3 - 1
        for z in range(SIZE_Z):
            for own in range(OWN):
                row = ROWS * pair + OWN * (z + 1 - c) + own
                tap_rows[z // 2, z % 2, own, tap, row] = 1.0
            for o in range(C_VEL):
                head_columns[pair, z + 2 - c, o, z, 32 * o + tap] = 1.0
    head_rows = np.zeros((32, 6, OWN), np.float32)
    for own in range(OWN):
        head_rows[27 + own, 1:5, own] = 1.0
    double = np.zeros((SIZE_X, SIZE_Y, SIZE_X // 2, SIZE_Y // 2), np.float32)
    for x in range(SIZE_X):
        for y in range(SIZE_Y):
            double[x, y, x // 2, y // 2] = 1.0
    return (
        jnp.asarray(tap_rows.reshape(2, 256, 216), BF16),
        jnp.asarray(head_columns.reshape(216, 512), BF16),
        jnp.asarray(head_rows.reshape(32, ROWS)),
        jnp.asarray(double.reshape(128, 32), BF16),
    )


def head_channels():
    rows = np.zeros((BLOCKS, 32, C_HID), np.float32)
    for at in range(BLOCKS):
        for own in range(OWN):
            rows[at, 27 + own, OWN * at + own] = 1.0
    return jnp.asarray(rows.reshape(512, C_HID), BF16)


def turn_kernel(pre_ref, cot_ref, rows_ref, high_ref, low_ref):
    turned = pre_ref[...].astype(F32).T.astype(BF16)
    rows_ref[0:256, :] = turned
    rows_ref[256:272, :] = cot_ref[...]
    high_ref[0:64, :] = turned[192:256]
    high_ref[64:80, :] = cot_ref[...]
    low_ref[0:64, :] = turned[0:64]
    low_ref[64:80, :] = cot_ref[...]


def joined(before_ref, rows_ref, after_ref, cot_choice_ref):
    pre = jnp.concatenate([before_ref[0:64, :], rows_ref[0:256, :], after_ref[0:64, :]], axis=0)
    cot = jnp.concatenate(
        [before_ref[64:80, :], rows_ref[256:272, :], after_ref[64:80, :]], axis=0
    )
    return pre, jnp.dot(cot_choice_ref[...], cot, preferred_element_type=F32)


def parts_kernel(before_ref, rows_ref, after_ref, choice_ref, cot_choice_ref, parts_ref):
    pre, cot = joined(before_ref, rows_ref, after_ref, cot_choice_ref)
    parts = jnp.dot(choice_ref[...], pre, preferred_element_type=F32)
    for at in range(BLOCKS):
        both = jnp.concatenate([parts[ROWS * at : ROWS * at + ROWS], cot[0:24]], axis=0)
        parts_ref[at] = both.astype(BF16)


def field_kernel(before_ref, rows_ref, after_ref, cot_choice_ref, field_ref):
    pre, cot = joined(before_ref, rows_ref, after_ref, cot_choice_ref)
    field = jnp.concatenate([pre.astype(F32), cot], axis=0).T
    field_ref[...] = field.astype(BF16).reshape(SIZE_X, SIZE_Y, 512)


def unpack_kernel(share_ref, choice_ref, body_ref, head_ref):
    for at in range(BLOCKS):
        wide = share_ref[at].astype(F32) * NORM
        body_ref[:, 768 * at : 768 * at + 768] = wide[0:27]
    rows = share_ref[:, :, 0:128].reshape(512, 128)
    head = lax.dot_general(
        rows, choice_ref[...], (((0,), (0,)), ((), ())), preferred_element_type=F32
    )
    for o in range(C_VEL):
        head_ref[o] = head[32 * o : 32 * o + 27] * NORM


def input_matrix(weight_one):
    taps = weight_one.reshape(9, 3, C_HID, 192)[:, ::-1].reshape(9, 192, 192)
    wide = jnp.concatenate([taps, taps[..., C_UP:]], axis=2)
    return jnp.pad(wide, ((0, 0), (0, 64), (0, 0)))


def low_half(shape):
    return lax.broadcasted_iota(jnp.int32, shape, len(shape) - 1) < 64


def rolled(values, shift):
    flat = values.reshape(-1, values.shape[-1])
    return pltpu.roll(flat, shift, 1).reshape(values.shape)


def moved_y(blocks, b, lane):
    if b == 0:
        return blocks
    out = []
    for at in range(BLOCKS):
        gx, gy = at // 4, at % 4
        there = blocks[4 * gx + (gy - b) % 4]
        edge = lane % 16 == (0 if b == 1 else 15)
        out.append(
            jnp.where(edge, pltpu.roll(there, -15 * b % 128, 1), pltpu.roll(blocks[at], b % 128, 1))
        )
    return out


def moved_x(blocks, a, lane):
    if a == 0:
        return blocks
    turned = [pltpu.roll(block, 16 * a % 128, 1) for block in blocks]
    edge = lane // 16 == (0 if a == 1 else 7)
    return [
        jnp.where(edge, turned[4 * ((at // 4 - a) % 4) + at % 4], turned[at])
        for at in range(BLOCKS)
    ]


def stack_moved(blocks, stack_ref):
    lane = lax.broadcasted_iota(jnp.int32, (ROWS, 128), 1)
    for b in (-1, 0, 1):
        rows = moved_y(blocks, b, lane)
        for a in (-1, 0, 1):
            start = ROWS * (3 * (a + 1) + b + 1)
            for at, block in enumerate(moved_x(rows, a, lane)):
                stack_ref[start : start + ROWS, 128 * at : 128 * at + 128] = block


def message_kernel(coarse_ref, skip_ref, parts_ref):
    for at in range(BLOCKS):
        parts_ref[at, 0:32, :] = coarse_ref[...]
        parts_ref[at, 32:160, :] = skip_ref[...]


def share_kernel(
    data_ref, input_ref, head_ref, tap_ref, column_ref, row_ref, double_ref, share_ref, stack_s, fine_s
):
    for at in range(BLOCKS):
        rows = slice(128 * at, 128 * at + 128)
        fine = jnp.dot(double_ref[...], input_ref[at, 0:32, :], preferred_element_type=F32)
        for pair in range(2):
            lanes = slice(128 * pair, 128 * pair + 128)
            fine_s[pair, rows, 0:128] = fine[:, lanes].astype(BF16)
            fine_s[pair, rows, 128:256] = input_ref[at, 32:160, lanes]

    blocks = [data_ref[at].astype(F32) for at in range(BLOCKS)]
    stack_moved([block[ROWS:48] for block in blocks], stack_s)
    cot = stack_s[...].astype(BF16)
    pre = jnp.concatenate([block[0:ROWS] for block in blocks], axis=1)
    d_hidden = jnp.dot(head_ref[...], cot, preferred_element_type=F32)
    d_pre = (d_hidden * gelu_slope(pre)).astype(BF16).astype(F32)
    hidden = gelu_value(pre).astype(BF16)
    pairs = lax.dot_general(hidden, cot, (((1,), (1,)), ((), ())), preferred_element_type=F32)
    spans = jnp.dot(
        pairs, column_ref[...].astype(F32), precision=HIGHEST, preferred_element_type=F32
    )
    depth = lax.broadcasted_iota(jnp.int32, (ROWS, 128), 0) // OWN
    kept = jnp.zeros((ROWS, 128), F32)
    for z in range(SIZE_Z):
        kept = jnp.where(depth == z + 1, spans[:, 128 * z : 128 * z + 128], kept)
    head = jnp.dot(row_ref[...], kept, precision=HIGHEST, preferred_element_type=F32)

    stack_moved([d_pre[:, 128 * at : 128 * at + 128] for at in range(BLOCKS)], stack_s)
    back = stack_s[...].astype(BF16)
    up = jnp.zeros((128, 128), F32)
    skip = jnp.zeros((128, 128), F32)
    for pair in range(2):
        result = jnp.dot(back, fine_s[pair], preferred_element_type=F32)
        taps = jnp.dot(
            tap_ref[pair].astype(F32), result, precision=HIGHEST, preferred_element_type=F32
        )
        up = up + taps[0:128, 0:128] + taps[128:256, 0:128]
        skip = skip + taps[0:128, 128:256] + rolled(taps[128:256, 128:256], 64)
    half = low_half((32, 128))
    for even in range(0, OWN, 2):
        first, second = slice(32 * even, 32 * even + 32), slice(32 * even + 32, 32 * even + 64)
        turned = rolled(up[second], 64)
        start = 192 * even
        share_ref[:, start : start + 128] = up[first] + head if even == 0 else up[first]
        share_ref[:, start + 128 : start + 256] = jnp.where(half, skip[first], turned)
        share_ref[:, start + 256 : start + 384] = jnp.where(half, turned, rolled(skip[second], 64))


def input_kernel(field_ref, head_ref, weight_ref, skip_ref, coarse_ref, cot_s, pre_s, window_s, sum_s):
    cot_s[:, 0:8, :] = jnp.zeros((12, 8, 128), F32)
    cot_s[:, 8:40, :] = field_ref[:, :, 384:512].astype(F32)
    total = jnp.zeros((240, 384), F32)
    for a in (-1, 0, 1):
        for b in (-1, 0, 1):
            moved = cot_s[1 - a : 11 - a, 8 - b : 32 - b, :].reshape(240, 128).astype(BF16)
            total = total + jnp.dot(
                moved[:, :32], head_ref[3 * (a + 1) + b + 1], preferred_element_type=F32
            )
    pre_wide = field_ref[1:11, :, 0:384].astype(F32)[:, :24].reshape(240, 384)
    d_pre = (total * gelu_slope(pre_wide)).astype(BF16).astype(F32)
    pre_s[...] = d_pre.reshape(10, 24, 384)

    half = low_half((10, 16, 128))
    for b in (-1, 0, 1):
        moved = pre_s[:, 2 - b : 18 - b, :]
        shifted = rolled(moved, 320)
        for z in range(SIZE_Z):
            source, start = (moved, 64 * z) if z % 2 == 0 else (shifted, 64 * z - 64)
            low = source[:, :, start : start + 128]
            high = jnp.where(half, source[:, :, start + 128 : start + 256], 0.0)
            window_s[b + 1, z, :, :, 0:128] = low.astype(BF16)
            window_s[b + 1, z, :, :, 128:256] = high.astype(BF16)

    windows = [
        window_s[b + 1, :, 1 - a : 9 - a].reshape(CELLS, 256)
        for a in (-1, 0, 1)
        for b in (-1, 0, 1)
    ]
    total = jnp.dot(
        jnp.concatenate(windows, axis=1),
        weight_ref[...].reshape(9 * 256, 256),
        preferred_element_type=F32,
    ).reshape(SIZE_Z, SIZE_X, SIZE_Y, 256)
    half = low_half((8, 16, 128))
    for pair in range(2):
        even, odd = total[2 * pair], total[2 * pair + 1]
        lanes = slice(128 * pair, 128 * pair + 128)
        skip_ref[:, :, lanes] = jnp.where(half, even[..., 128:], odd[..., 128:]).astype(BF16)
        both = (even[..., :128] + odd[..., :128]).reshape(4, 2, 16, 128)
        sum_s[...] = (both[:, 0] + both[:, 1]).reshape(64, 128)
        summed = sum_s[pl.ds(0, 32, stride=2), :] + sum_s[pl.ds(1, 32, stride=2), :]
        coarse_ref[:, lanes] = summed.astype(BF16)


def traded(parts, axes):
    return lax.all_to_all(parts, axes, 0, 0)


def spread(part, axes):
    peers = lax.axis_size(axes)
    return traded(jnp.broadcast_to(part[None], (peers, *part.shape)), axes)


def per_device(coarse, skip_features, pre_act, cotangent, weight_one, weight_out):
    inputs = plane_inputs(coarse, skip_features)
    head = head_matrix(weight_out)
    deep = depth_rims(pre_act, cotangent)
    share_choice, cot_choice = row_choices()
    parts = pl.pallas_call(
        parts_kernel,
        out_shape=jax.ShapeDtypeStruct((BLOCKS, 48, 128), BF16),
        compiler_params=pltpu.CompilerParams(vmem_limit_bytes=8 * 2**20),
    )(*deep, share_choice, cot_choice)
    parts, inputs = lax.optimization_barrier((parts, inputs))
    data = traded(parts, PLANE)
    field = pl.pallas_call(
        field_kernel,
        out_shape=jax.ShapeDtypeStruct((SIZE_X, SIZE_Y, 512), BF16),
        compiler_params=pltpu.CompilerParams(vmem_limit_bytes=8 * 2**20),
        cost_estimate=pl.CostEstimate(
            flops=60_000_000, bytes_accessed=4_000_000, transcendentals=0
        ),
    )(*deep, cot_choice)
    data, field = lax.optimization_barrier((data, field))
    share = pl.pallas_call(
        share_kernel,
        out_shape=jax.ShapeDtypeStruct(SHARE, F32),
        scratch_shapes=[pltpu.VMEM((216, 2048), F32), pltpu.VMEM((2, 2048, 256), BF16)],
        compiler_params=pltpu.CompilerParams(vmem_limit_bytes=32 * 2**20),
        cost_estimate=pl.CostEstimate(
            flops=1_500_000_000, bytes_accessed=2_000_000, transcendentals=200_000
        ),
    )(data, inputs, own_head_matrix(head), *choices())
    near = jnp.sum(traded(share.reshape(4, 8, SHARE[1]), NEAR), axis=0)
    field, near = lax.optimization_barrier((field, near))
    field = with_x_rims(field)
    far = jnp.sum(spread(near.astype(BF16), FAR).astype(F32), axis=0)
    column = spread(far.astype(BF16), NEAR).reshape(SHARE)
    weights = input_matrix(weight_one)
    field, column, weights = lax.optimization_barrier((field, column, weights))
    field = with_y_rims(field)
    body, head_grad = pl.pallas_call(
        unpack_kernel,
        out_shape=(
            jax.ShapeDtypeStruct((27, C_HID * 192), F32),
            jax.ShapeDtypeStruct((C_VEL, 27, C_HID), F32),
        ),
        compiler_params=pltpu.CompilerParams(vmem_limit_bytes=16 * 2**20),
    )(spread(column, PLANE), head_channels())
    skip_grad, coarse_grad = pl.pallas_call(
        input_kernel,
        out_shape=(
            jax.ShapeDtypeStruct((SIZE_X, SIZE_Y, 256), BF16),
            jax.ShapeDtypeStruct((32, 256), BF16),
        ),
        scratch_shapes=[
            pltpu.VMEM((12, 40, 128), F32),
            pltpu.VMEM((10, 24, 384), F32),
            pltpu.VMEM((3, SIZE_Z, 10, 16, 256), BF16),
            pltpu.VMEM((64, 128), F32),
        ],
        compiler_params=pltpu.CompilerParams(vmem_limit_bytes=32 * 2**20),
        cost_estimate=pl.CostEstimate(
            flops=700_000_000, bytes_accessed=3_000_000, transcendentals=100_000
        ),
    )(field, head, weights)
    return coarse_grad.reshape(4, 8, 256), skip_grad, body, jnp.transpose(head_grad, (1, 0, 2))


def solution(mesh):
    names = ("gx", "gy", "gzh", "gzm", "gzl")
    split = Mesh(mesh.devices.reshape(4, 4, 2, 8, 2), names)
    field = P("gx", "gy", GZ)
    return jax.shard_map(
        per_device,
        mesh=split,
        in_specs=(field, field, field, P(None, "gx", "gy", GZ), P(), P()),
        out_specs=(field, field, P(), P()),
        check_vma=False,
    )
```
